32 devices in a mesh: ctx: 8 (over z, core), fsdp: 4 (over y, x).
Axes of the slice: x: 2, y: 2, z: 4, core: 2. Of those that a mesh axis runs over, the one named last changes fastest.
Arguments:
- tokens: bfloat16 [4, 1024, 1536], P('fsdp', 'ctx'), may hold values from -6 to 6
- segments: int32 [4, 1024], P('fsdp', 'ctx'), may hold values from 0 to 11, as said below
- positions: int32 [4, 1024], P('fsdp', 'ctx'), may hold values from 0 to 511, as said below
- norm1_gain: bfloat16 [1536], P(('ctx', 'fsdp')), may hold values from 0.5 to 1.5
- qkv_weight: bfloat16 [1536, 2048], P(('ctx', 'fsdp')), may hold values from -0.21875 to 0.21875
- qkv_bias: bfloat16 [2048], P(('ctx', 'fsdp')), may hold values from -3 to 3
- out_weight: bfloat16 [1536, 1536], P(('ctx', 'fsdp')), may hold values from -0.5 to 0.5
- norm2_gain: bfloat16 [1536], P(('ctx', 'fsdp')), may hold values from 0.5 to 1.5
- gate_up_weight: bfloat16 [1536, 17920], P(('ctx', 'fsdp')), may hold values from -0.15625 to 0.15625
- down_weight: bfloat16 [8960, 1536], P(('ctx', 'fsdp')), may hold values from -0.125 to 0.125
- cotangent: bfloat16 [4, 1024, 1536], P('fsdp', 'ctx'), may hold values from -6 to 6
Outputs:
- output: bfloat16 [4, 1024, 1536], P('fsdp', 'ctx')
- input_grad: float32 [4, 1024, 1536], P('fsdp', 'ctx')
- norm1_grad: float32 [1536], P(('ctx', 'fsdp'))
- qkv_weight_grad: float32 [1536, 2048], P(('ctx', 'fsdp'))
- qkv_bias_grad: float32 [2048], P(('ctx', 'fsdp'))
- out_weight_grad: float32 [1536, 1536], P(('ctx', 'fsdp'))
- norm2_grad: float32 [1536], P(('ctx', 'fsdp'))
- gate_up_grad: float32 [1536, 17920], P(('ctx', 'fsdp'))
- down_grad: float32 [8960, 1536], P(('ctx', 'fsdp'))
The draws below stay inside these ranges and needn't reach their ends.
Inputs may be any that keep to these rules, and one draw needn't show every extreme that they name: `segments`: within each sequence documents are numbered 0, 1, 2 and so on in order; each whole document has 51 to 512 tokens, the last one may be cut by the sequence's end, and one of the first two has exactly 512. `positions`: A token's place within its document, 0 at the document's first token.
All inputs are finite; a program needn't handle non-finite values.
Results may differ from the reference program's by a relative error of at most 0.033.
Values may be sent and summed in bfloat16 or wider, within the bound.
No kernel may reach another device: no remote copies, remote signals or barrier semaphores. Data moves between devices by JAX's collectives and lax.ppermute only.
A program may use at most 512 MiB of HBM per device.

```python
import math
import jax
import jax.numpy as jnp
from jax import lax

D = 1536
FF = 8960
Q_HEADS = 12
KV_HEADS = 2
HEAD_DIM = 128
QKV_WIDTH = 2048
SEQ_LEN = 1024
SEQ_COUNT = 4
DOC_MOST = 512
DOC_LEAST = 51
DOC_SLOTS = 21


def document_layout(key):
    base = jax.random.fold_in(key, 17)
    seq_keys = jax.random.split(base, SEQ_COUNT)
    seq_numbers = jnp.arange(SEQ_COUNT, dtype=jnp.int32)

    def one_sequence(seq_key, seq_number):
        length_key, pick_key = jax.random.split(seq_key)
        lengths = jax.random.randint(length_key, (DOC_SLOTS,), DOC_LEAST, DOC_MOST + 1)
        lengths = jnp.where(seq_number == 0, DOC_LEAST, lengths)
        chosen = jax.random.randint(pick_key, (), 0, 2)
        lengths = jnp.where(jnp.arange(DOC_SLOTS, dtype=jnp.int32) == chosen, DOC_MOST, lengths)
        ends = jnp.cumsum(lengths)
        starts = ends - lengths
        places = jnp.arange(SEQ_LEN, dtype=jnp.int32)
        numbers = jnp.sum((places[:, None] >= ends[None, :]).astype(jnp.int32), axis=1)
        begins = jnp.max(jnp.where(starts[None, :] <= places[:, None], starts[None, :], 0), axis=1)
        return (numbers.astype(jnp.int32), (places - begins).astype(jnp.int32))
    return jax.vmap(one_sequence)(seq_keys, seq_numbers)


def draw_segments(key, part):
    return document_layout(key)[0]


def draw_positions(key, part):
    return document_layout(key)[1]


def block_levels(key, dims, cuts, least, top_value):
    factor_of, own = 1.0, jax.random.fold_in(key, 6)
    for position, blocks in cuts:
        draws = jnp.exp(jax.random.uniform(jax.random.fold_in(own, position), (blocks,), jnp.float32, least / len(cuts), top_value / len(cuts)))
        factor_of = factor_of * jnp.repeat(draws, dims[position] // blocks).reshape([-1 if axis == position else 1 for axis in range(len(dims))])
    return factor_of


def scatter_about(key, shape, deviation, most, shards=(), held_as=jnp.bfloat16):
    level = block_levels(key, shape, shards, -0.22, 0.18) if shards else 1.0
    array = jax.random.normal(key, shape, jnp.float32) * deviation * level
    return jnp.minimum(jnp.maximum(array, -most), most).astype(held_as)


def setup_inputs(seed: int = 0) -> dict:
    streams_of = jax.random.split(jax.random.key(seed), 12)
    tokens = scatter_about(streams_of[0], (SEQ_COUNT, SEQ_LEN, D), 1.0, 6.0, ((0, 4), (1, 8)))
    segments = draw_segments(jax.random.fold_in(streams_of[11], 71), 0)
    positions = draw_positions(jax.random.fold_in(streams_of[11], 71), 0)
    norm1_gain = jnp.clip(1.0 + 0.1 * jax.random.normal(streams_of[3], (D,), jnp.float32), 0.5, 1.5).astype(jnp.bfloat16)
    qkv_weight = scatter_about(streams_of[4], (D, QKV_WIDTH), (D // 2) ** -0.5, 0.21875, ((0, 32),))
    qkv_bias = scatter_about(streams_of[5], (QKV_WIDTH,), 0.5, 3.0, ((0, 32),))
    out_weight = scatter_about(streams_of[6], (D, Q_HEADS * HEAD_DIM), (Q_HEADS * HEAD_DIM // 12) ** -0.5, 0.5, ((0, 32),))
    norm2_gain = jnp.clip(1.0 + 0.1 * jax.random.normal(streams_of[7], (D,), jnp.float32), 0.5, 1.5).astype(jnp.bfloat16)
    gate_up_weight = scatter_about(streams_of[8], (D, 2 * FF), D ** -0.5, 0.15625, ((0, 32),))
    down_weight = scatter_about(streams_of[9], (FF, D), (FF // 4) ** -0.5, 0.125, ((0, 32),))
    cotangent = scatter_about(streams_of[10], (SEQ_COUNT, SEQ_LEN, D), 1.0, 6.0, ((0, 4), (1, 8)))
    return {"tokens": tokens, "segments": segments, "positions": positions, "norm1_gain": norm1_gain, "qkv_weight": qkv_weight, "qkv_bias": qkv_bias, "out_weight": out_weight, "norm2_gain": norm2_gain, "gate_up_weight": gate_up_weight, "down_weight": down_weight, "cotangent": cotangent}


EPSILON = 1e-06
HIGHEST = lax.Precision.HIGHEST

@jax.custom_vjp
def low(v):
    return lax.optimization_barrier(v.astype(jnp.bfloat16)).astype(jnp.float32)

@jax.custom_vjp
def low_back(v):
    return v

def low_keep(v):
    return (low(v), None)

def low_pass(kept, grad):
    return (grad,)

def back_keep(v):
    return (v, None)

def back_low(kept, grad):
    return (low(grad),)
low.defvjp(low_keep, low_pass)
low_back.defvjp(back_keep, back_low)

def rms_norm(values_in, gain):
    factor = lax.rsqrt(lax.optimization_barrier(jnp.mean(values_in * values_in, axis=-1, keepdims=True)) + EPSILON)
    return values_in * factor * gain

def angle_tables(place_ids):
    steps_half = jnp.arange(0, HEAD_DIM, 2).astype(jnp.float32)
    inverse = 10000.0 ** (-steps_half / HEAD_DIM)
    turns = place_ids.astype(jnp.float32)[:, None] * inverse[None, :]
    turns = jnp.concatenate([turns, turns], axis=-1)
    return (jnp.cos(turns), jnp.sin(turns))

def rotate(heads_in, cosine, sine):
    half = heads_in.shape[-1] // 2
    turned = jnp.concatenate([-heads_in[..., half:], heads_in[..., :half]], axis=-1)
    return heads_in * cosine[:, None, :] + turned * sine[:, None, :]

def attend(queries, key_heads, values, segment_ids):
    length = queries.shape[0]
    block_rows = math.gcd(512, length)
    group_size = Q_HEADS // KV_HEADS
    wide_keys = jnp.repeat(key_heads, group_size, axis=1)
    wide_values = jnp.repeat(values, group_size, axis=1)
    places = jnp.arange(length, dtype=jnp.int32)
    score_scale = HEAD_DIM ** (-0.5)

    def one_block(block_index):
        first = (block_index * block_rows).astype(jnp.int32)
        query_block = lax.dynamic_slice_in_dim(queries, first, block_rows, 0)
        query_seg = lax.dynamic_slice_in_dim(segment_ids, first, block_rows, 0)
        query_place = lax.dynamic_slice_in_dim(places, first, block_rows, 0)
        scores = jnp.einsum('qhd,khd->hqk', query_block, wide_keys, precision=HIGHEST) * score_scale
        scores = low_back(scores)
        allowed = (query_seg[:, None] == segment_ids[None, :]) & (query_place[:, None] >= places[None, :])
        scores = jnp.where(allowed[None], scores, -jnp.inf)
        probability = low(jax.nn.softmax(scores, axis=-1))
        return jnp.einsum('hqk,khd->qhd', probability, wide_values, precision=HIGHEST)
    outputs = lax.map(jax.checkpoint(one_block), jnp.arange(length // block_rows, dtype=jnp.int32))
    return outputs.reshape(length, Q_HEADS, HEAD_DIM)

def layer(inputs, segment_ids, place_ids, gain_one, w_qkv, b_qkv, w_out, gain_two, w_gate_up, w_down):
    length = inputs.shape[0]
    width_q = Q_HEADS * HEAD_DIM
    width_k = KV_HEADS * HEAD_DIM
    normed_one = low(rms_norm(inputs, gain_one))
    projected = low_back(jnp.dot(normed_one, w_qkv, precision=HIGHEST) + b_qkv)
    cosine, sine = angle_tables(place_ids)
    queries = low(rotate(projected[:, :width_q].reshape(length, Q_HEADS, HEAD_DIM), cosine, sine))
    key_heads = low(rotate(projected[:, width_q:width_q + width_k].reshape(length, KV_HEADS, HEAD_DIM), cosine, sine))
    values = low(projected[:, width_q + width_k:].reshape(length, KV_HEADS, HEAD_DIM))
    context = attend(queries, key_heads, values, segment_ids).reshape(length, width_q)
    context = low(low_back(context))
    attention = low_back(lax.dot_general(context, w_out, (((1,), (1,)), ((), ())), precision=HIGHEST))
    middle = inputs + attention
    normed_two = low(rms_norm(middle, gain_two))
    gate_up = low_back(jnp.dot(normed_two, w_gate_up, precision=HIGHEST))
    hidden = low(jax.nn.silu(gate_up[:, :FF]) * gate_up[:, FF:])
    branch = low_back(jnp.dot(hidden, w_down, precision=HIGHEST))
    return middle + branch

def reference(tokens, segments, positions, norm1_gain, qkv_weight, qkv_bias, out_weight, norm2_gain, gate_up_weight, down_weight, cotangent):
    weight_list = tuple((member.astype(jnp.float32) for member in (norm1_gain, qkv_weight, qkv_bias, out_weight, norm2_gain, gate_up_weight, down_weight)))

    def one_sequence(totals, item):
        inputs, segment_ids, place_ids, grad_in = item

        def forward(inputs_f, *weights_f):
            return layer(inputs_f, segment_ids, place_ids, *weights_f)
        result, pull = jax.vjp(forward, inputs.astype(jnp.float32), *weight_list)
        grads = pull(grad_in.astype(jnp.float32))
        totals = tuple((total + grad for total, grad in zip(totals, grads[1:])))
        return (totals, (result.astype(jnp.bfloat16), grads[0]))
    zeros = tuple((jnp.zeros_like(member) for member in weight_list))
    totals, (outputs, input_grads) = lax.scan(one_sequence, zeros, (tokens, segments, positions, cotangent))
    return (outputs, input_grads, totals[0], totals[1], totals[2], totals[3], totals[4], totals[5], totals[6])
```

```python
import functools

import jax
import jax.numpy as jnp
from jax import lax
from jax.experimental import pallas as pl
from jax.experimental.pallas import tpu as pltpu
from jax.sharding import PartitionSpec as P

Q_HEADS = 12
KV_HEADS = 2
HEAD_DIM = 128
GROUP = Q_HEADS // KV_HEADS
WIDTH_Q = Q_HEADS * HEAD_DIM
WIDTH_K = KV_HEADS * HEAD_DIM
QKV = WIDTH_Q + 2 * WIDTH_K
LANES = 128
ROW_TILE = 16
EPSILON = 1e-06
SCALE = HEAD_DIM ** (-0.5)
BF16 = jnp.bfloat16
F32 = jnp.float32
VMEM_LIMIT = 56 * 1024 * 1024
BOTH = ("ctx", "fsdp")

SMEM_SPEC = pl.BlockSpec(memory_space=pltpu.SMEM)
VMEM_SPEC = pl.BlockSpec(memory_space=pltpu.VMEM)
ANY_SPEC = pl.BlockSpec(memory_space=pl.ANY)


def dot_nn(left, right):
    return lax.dot_general(left, right, (((1,), (0,)), ((), ())), preferred_element_type=F32)


def dot_tn(left, right):
    return lax.dot_general(left, right, (((0,), (0,)), ((), ())), preferred_element_type=F32)


def dot_nt(left, right):
    return lax.dot_general(left, right, (((1,), (1,)), ((), ())), preferred_element_type=F32)


def params():
    return pltpu.CompilerParams(vmem_limit_bytes=VMEM_LIMIT)


def cost(flops, nbytes, exps=0):
    return pl.CostEstimate(flops=int(flops), bytes_accessed=int(nbytes), transcendentals=int(exps))


def struct(shape, dtype):
    return jax.ShapeDtypeStruct(shape, dtype)


def swap_core(value):
    count = lax.axis_size("ctx")
    return lax.ppermute(value, "ctx", [(i, i ^ 1) for i in range(count)])


def shift_chip(value, steps):
    count = lax.axis_size("ctx")
    return lax.ppermute(value, "ctx", [(i, (i + 2 * steps) % count) for i in range(count)])


def shift_open(value, steps):
    count = lax.axis_size("ctx")
    pairs = [(i, i + 2 * steps) for i in range(count) if 0 <= i + 2 * steps < count]
    return lax.ppermute(value, "ctx", pairs)


def send_to(value, steps, other):
    count = lax.axis_size("ctx")
    return lax.ppermute(
        value, "ctx", [(i, ((i + 2 * steps) % count) ^ other) for i in range(count)]
    )


def swap_fsdp(value, bit):
    count = lax.axis_size("fsdp")
    return lax.ppermute(value, "fsdp", [(i, i ^ bit) for i in range(count)])


def picked(array, numbers, axis):
    items = [
        lax.dynamic_index_in_dim(array, numbers[index], axis, keepdims=False)
        for index in range(numbers.shape[0])
    ]
    return jnp.stack(items, axis=axis)


def bits_of(count):
    return [1 << k for k in range(count.bit_length() - 1)]


def halving_order(bits):
    if not bits:
        return [0]
    rest = halving_order(bits[1:])
    return [bits[0] ^ item for item in rest] + rest


def halves_of(chips, fsdp):
    bits = bits_of(fsdp)
    near = [step for step in range(chips) if step in (0, 1)]
    if chips > 2:
        far = [step for step in range(chips) if step not in near]
        return [(near, bits), (far, bits[::-1])]
    return [(near, bits)]


def gather_blocks(shard, chips, fsdp):
    if shard.shape[0] % ROW_TILE:
        return [lax.all_gather(shard, BOTH, axis=0, tiled=True)], None
    moved = {0: shard}
    for step in [1, chips - 1] + list(range(2, chips - 1)):
        if step not in moved and step < chips:
            moved[step] = shift_chip(shard, step)
    arrays, plan = [], []
    for steps, bits in halves_of(chips, fsdp):
        held = {0: jnp.concatenate([moved[step] for step in steps], axis=0)}
        for bit in bits:
            for item in list(held):
                held[item ^ bit] = swap_fsdp(held[item], bit)
        for item, array in held.items():
            for other, version in ((0, array), (1, swap_core(array))):
                for block, step in enumerate(steps):
                    plan.append((len(arrays), block, step, other, item))
                arrays.append(version)
    return arrays, plan


def reduce_blocks(kept, sent, chips, fsdp):
    if not sent:
        return lax.psum_scatter(kept[0], BOTH, scatter_dimension=0, tiled=True).astype(F32)
    total = None
    for (steps, bits), keep, send in zip(halves_of(chips, fsdp), kept, sent):
        held = keep + swap_core(send)
        for bit in bits:
            half = held.shape[0] // 2
            held = held[half:] + swap_fsdp(held[:half], bit)
        held = held[0]
        for at, step in enumerate(steps):
            part = held[at] if step == 0 else shift_chip(held[at], step)
            part = part.astype(F32)
            total = part if total is None else total + part
    return total


def block_row(info_ref, chips, fsdp, step, other, item, away=-1):
    chip = info_ref[0] // 2
    core = info_ref[0] % 2
    chip = (chip + away * step + chips) % chips
    core = 1 - core if other else core
    return (2 * chip + core) * fsdp + jnp.bitwise_xor(info_ref[1], item)


def copies_of(plan, info_ref, pieces, whole, sems, rows, columns, chips, fsdp):
    if plan is None:
        source = pieces[0].at[:, pl.ds(columns[0], columns[1])]
        return [pltpu.make_async_copy(source, whole, sems.at[0])]
    copies = []
    for index, (array, block, step, other, item) in enumerate(plan):
        row = block_row(info_ref, chips, fsdp, step, other, item) * rows
        row = pl.multiple_of(row, rows)
        source = pieces[array].at[pl.ds(block * rows, rows), pl.ds(columns[0], columns[1])]
        copies.append(pltpu.make_async_copy(source, whole.at[pl.ds(row, rows)], sems.at[index]))
    return copies


def normalised(values):
    return lax.rsqrt(jnp.mean(values * values, axis=-1, keepdims=True) + EPSILON)


def pack_kernel(qkv_ref, bias_ref, out_ref, gain_ref, packed_ref):
    packed_ref[:, :QKV] = (qkv_ref[...].astype(F32) * gain_ref[...]).astype(BF16)
    packed_ref[:, QKV : QKV + LANES] = bias_ref[...]
    packed_ref[:, QKV + LANES :] = out_ref[...]


def split_kernel(chips, own, padded, info_ref, weight_ref, gain_ref, split_ref):
    total = weight_ref.shape[1] // 2
    count = 2 * chips
    rows = weight_ref.shape[0]
    chip = info_ref[0] // 2
    core = info_ref[0] % 2
    filler = jnp.zeros((rows, padded - own), F32)
    for target in range(count):
        step = (target // 2 - chip + chips) % chips
        other = jnp.bitwise_xor(core, target % 2)
        for part in range(2):
            start = part * total + target * own
            values = weight_ref[:, start : start + own].astype(F32) * gain_ref[...]
            if padded > own:
                values = jnp.concatenate([values, filler], axis=1)
            split_ref[other, step, :, part * padded : (part + 1) * padded] = values.astype(BF16)


def join_kernel(chips, own, padded, info_ref, parts_ref, weight_ref, gain_ref, grad_ref, norm_ref):
    total = weight_ref.shape[1] // 2
    rows = weight_ref.shape[0]
    chip = info_ref[0] // 2
    core = info_ref[0] % 2
    sums = jnp.zeros((rows, 1), F32)
    for source in range(2 * chips):
        step = (chip - source // 2 + chips) % chips
        other = jnp.bitwise_xor(core, source % 2)
        for part in range(2):
            values = parts_ref[other * chips + step, :, part * padded : (part + 1) * padded]
            values = values[:, :own].astype(F32)
            start = part * total + source * own
            grad_ref[:, start : start + own] = values * gain_ref[...]
            sums = sums + jnp.sum(
                values * weight_ref[:, start : start + own].astype(F32), axis=1, keepdims=True
            )
    norm_ref[...] = sums


def project_kernel(plan, chips, fsdp, bias_width, count, info_ref, tokens_ref, cos_ref, sin_ref, *refs):
    pieces = refs[:count]
    unit_ref, q_ref, kv_ref, whole, sems = refs[count:]
    width = tokens_ref.shape[1]
    rows = width // (2 * chips * fsdp)
    copies = copies_of(plan, info_ref, pieces, whole, sems, rows, (0, QKV + LANES), chips, fsdp)
    for copy in copies:
        copy.start()
    values = tokens_ref[...].astype(F32)
    unit = (values * normalised(values)).astype(BF16)
    unit_ref[...] = unit
    for copy in copies:
        copy.wait()
    cosine, sine = cos_ref[...], sin_ref[...]
    each = LANES // bias_width
    for tile in range(QKV // LANES):
        at = tile * LANES
        bias = jnp.zeros((1, LANES), F32)
        for member in range(each):
            block = (tile * each + member) * rows
            first = block // ROW_TILE * ROW_TILE
            group = whole[first : first + ROW_TILE, QKV:].astype(F32)
            bias = bias + group[block - first : block - first + 1]
        head = dot_nn(unit, whole[:, at : at + LANES]) + bias
        if at < WIDTH_Q + WIDTH_K:
            head = head * cosine + pltpu.roll(head, HEAD_DIM // 2, 1) * sine
        if at < WIDTH_Q:
            q_ref[:, at : at + LANES] = head.astype(BF16)
        else:
            kv_ref[:, at - WIDTH_Q : at - WIDTH_Q + LANES] = head.astype(BF16)


def key_mask(info_ref, place_ref, rows, sources):
    own = info_ref[0] * rows + lax.broadcasted_iota(jnp.int32, (rows, rows), 0)
    begin = own - place_ref[...]
    masks = []
    for step, other in sources:
        block = info_ref[0] - 2 * step
        if other:
            block = jnp.bitwise_xor(info_ref[0], 1) - 2 * step
        keys = block * rows + lax.broadcasted_iota(jnp.int32, (rows, rows), 1)
        masks.append((keys <= own) & (keys >= begin) & (keys >= 0))
    return jnp.concatenate(masks, axis=1)


def head_part(kv_refs, column):
    return jnp.concatenate([ref[:, column : column + HEAD_DIM] for ref in kv_refs], axis=0)


def probabilities(query, keys, allowed):
    scores = dot_nt(query, keys) * SCALE
    scores = jnp.where(allowed, scores, -1e30)
    exps = jnp.exp(scores - jnp.max(scores, axis=1, keepdims=True))
    return exps * (1.0 / jnp.sum(exps, axis=1, keepdims=True))


def attend_kernel(plan, chips, fsdp, count, sources, info_ref, place_ref, q_ref, tokens_ref, *refs):
    kv_refs = refs[: len(sources)]
    refs = refs[len(sources) :]
    pieces = refs[:count]
    context_ref, middle_ref, unit_ref, whole, sems = refs[count:]
    rows, width = tokens_ref.shape
    block_rows = width // (2 * chips * fsdp)
    copies = copies_of(
        plan, info_ref, pieces, whole, sems, block_rows, (QKV + LANES, width), chips, fsdp
    )
    for copy in copies:
        copy.start()
    allowed = key_mask(info_ref, place_ref, rows, sources)
    for kv_head in range(KV_HEADS):
        keys = head_part(kv_refs, kv_head * HEAD_DIM)
        values = head_part(kv_refs, WIDTH_K + kv_head * HEAD_DIM)
        for member in range(GROUP):
            at = (kv_head * GROUP + member) * HEAD_DIM
            probs = probabilities(q_ref[:, at : at + HEAD_DIM], keys, allowed).astype(BF16)
            context_ref[:, at : at + HEAD_DIM] = dot_nn(probs, values).astype(BF16)
    for copy in copies:
        copy.wait()
    middle = tokens_ref[...].astype(F32) + dot_nt(context_ref[...], whole[...])
    middle_ref[...] = middle
    unit_ref[...] = (middle * normalised(middle)).astype(BF16)


def feed_kernel(
    chips, fsdp, own, padded, info_ref, x_mine, x_other, c_mine, c_other, wide_ref, down_ref,
    gu_mine, gu_other, br_mine, br_other, hidden_ref, grad_ref,
    wide, down, acc_units, acc_branch, sems,
):
    rows, width = x_mine.shape
    block_rows = width // (2 * chips * fsdp)
    copies = []
    index = 0
    if block_rows % ROW_TILE:
        copies.append(pltpu.make_async_copy(wide_ref, wide, sems.at[0]))
        index = 1
    for item in range(0 if index else fsdp):
        for other in range(2):
            for step in range(chips):
                chip = (info_ref[0] // 2 - step + chips) % chips
                core = jnp.bitwise_xor(info_ref[0] % 2, other)
                row = pl.multiple_of(((2 * chip + core) * fsdp + item) * block_rows, block_rows)
                copies.append(
                    pltpu.make_async_copy(
                        wide_ref.at[item, other * chips + step],
                        wide.at[pl.ds(row, block_rows)],
                        sems.at[index],
                    )
                )
                index += 1
    last = pltpu.make_async_copy(down_ref, down.at[pl.ds(0, own)], sems.at[index])
    for copy in copies:
        copy.start()
    last.start()
    if padded > own:
        down[own:, :] = jnp.zeros((padded - own, width), BF16)
    for copy in copies:
        copy.wait()
    last.wait()
    x = jnp.concatenate([x_mine[...], x_other[...]], axis=0)
    c = jnp.concatenate([c_mine[...], c_other[...]], axis=0)
    block = 384 if padded % 384 == 0 else LANES
    for at in range(0, padded, block):
        span = slice(at, at + block)
        span_up = slice(padded + at, padded + at + block)
        gate = dot_nn(x, wide[:, span])
        up = dot_nn(x, wide[:, span_up])
        grad_hidden = dot_nt(c, down[span, :])
        sig = 1.0 / (1.0 + jnp.exp(-gate))
        swished = gate * sig
        hidden = (swished * up).astype(BF16)
        grad_gate = (grad_hidden * up * sig * (1.0 + gate * (1.0 - sig))).astype(BF16)
        grad_up = (grad_hidden * swished).astype(BF16)
        hidden_ref[:, span] = hidden
        grad_ref[:, span] = grad_gate
        grad_ref[:, span_up] = grad_up
        units = dot_nt(grad_gate, wide[:, span]) + dot_nt(grad_up, wide[:, span_up])
        branch = dot_nn(hidden, down[span, :])
        if at == 0:
            acc_units[...] = units
            acc_branch[...] = branch
        else:
            acc_units[...] += units
            acc_branch[...] += branch
    gu_mine[...] = acc_units[:rows].astype(BF16)
    gu_other[...] = acc_units[rows:].astype(BF16)
    br_mine[...] = acc_branch[:rows].astype(BF16)
    br_other[...] = acc_branch[rows:].astype(BF16)


def wide_grad_kernel(chips, fsdp, n_units, info_ref, *refs):
    units = refs[:n_units]
    grads = refs[n_units : n_units + n_units // 2]
    out_ref, turned, total = refs[n_units + n_units // 2 :]
    rows, width = units[0].shape
    block_rows = width // (2 * chips * fsdp)

    @pl.when(pl.program_id(0) == 0)
    def _():
        for index, unit in enumerate(units):
            turned[:, index * rows : (index + 1) * rows] = unit[...].T

    for index, grad in enumerate(grads):
        part = dot_nn(turned[:, index * 2 * rows : (index + 1) * 2 * rows], grad[...])
        if index == 0:
            total[...] = part
        else:
            total[...] += part
    if block_rows % ROW_TILE:
        out_ref[...] = total[...].astype(BF16)
        return
    for item in range(fsdp):
        for other in range(2):
            for step in range(chips):
                chip = (info_ref[0] // 2 + step) % chips
                core = jnp.bitwise_xor(info_ref[0] % 2, other)
                row = pl.multiple_of(((2 * chip + core) * fsdp + item) * block_rows, block_rows)
                out_ref[item, other * chips + step] = total[pl.ds(row, block_rows), :].astype(BF16)


def down_grad_kernel(own, n_hidden, *refs):
    hiddens = refs[:n_hidden]
    cots = refs[n_hidden : 3 * n_hidden]
    out_ref, turned = refs[3 * n_hidden :]
    rows = hiddens[0].shape[0]

    @pl.when(pl.program_id(0) == 0)
    def _():
        for index, hidden in enumerate(hiddens):
            turned[:, index * rows : (index + 1) * rows] = hidden[...].T

    total = None
    for index in range(n_hidden):
        c = jnp.concatenate([cots[2 * index][...], cots[2 * index + 1][...]], axis=0)
        part = dot_nn(turned[:own, index * rows : (index + 1) * rows], c)
        total = part if total is None else total + part
    out_ref[...] = total.astype(BF16)


def middle_back_kernel(
    plan, chips, fsdp, count, sources, info_ref, place_ref, q_ref, own_ref, came_ref, middle_ref, cot_ref, *refs
):
    kv_refs = refs[: len(sources)]
    refs = refs[len(sources) :]
    pieces = refs[:count]
    grad_ref, att_ref, dq_ref, mine_ref, other_ref, whole, sems = refs[count:]
    rows, width = middle_ref.shape
    block_rows = width // (2 * chips * fsdp)
    copies = copies_of(
        plan, info_ref, pieces, whole, sems, block_rows, (QKV + LANES, width), chips, fsdp
    )
    for copy in copies:
        copy.start()
    units = own_ref[...].astype(F32) + came_ref[...].astype(F32)
    middle = middle_ref[...]
    rms = normalised(middle)
    grad_middle = (
        cot_ref[...].astype(F32)
        + rms * units
        - middle * (rms * rms * rms) * jnp.mean(units * middle, axis=-1, keepdims=True)
    )
    grad_ref[...] = grad_middle
    attention = grad_middle.astype(BF16)
    att_ref[...] = attention
    allowed = key_mask(info_ref, place_ref, rows, sources)
    for copy in copies:
        copy.wait()
    context_grad = dot_nn(attention, whole[...]).astype(BF16)
    for kv_head in range(KV_HEADS):
        keys = head_part(kv_refs, kv_head * HEAD_DIM)
        values = head_part(kv_refs, WIDTH_K + kv_head * HEAD_DIM)
        dkey = None
        dvalue = None
        for member in range(GROUP):
            at = (kv_head * GROUP + member) * HEAD_DIM
            query = q_ref[:, at : at + HEAD_DIM]
            grad = context_grad[:, at : at + HEAD_DIM]
            probs = probabilities(query, keys, allowed)
            dprobs = dot_nt(grad, values)
            offset = jnp.sum(probs * dprobs, axis=1, keepdims=True)
            dscores = (probs * (dprobs - offset)).astype(BF16)
            dq_ref[:, at : at + HEAD_DIM] = dot_nn(dscores, keys) * SCALE
            more_key = dot_tn(dscores, query)
            more_value = dot_tn(probs.astype(BF16), grad)
            dkey = more_key if dkey is None else dkey + more_key
            dvalue = more_value if dvalue is None else dvalue + more_value
        dkey = (dkey * SCALE).astype(BF16)
        dvalue = dvalue.astype(BF16)
        for index, (step, other) in enumerate(sources):
            ref = other_ref if other else mine_ref
            span = slice(index * rows, (index + 1) * rows)
            ref[step, :, kv_head * HEAD_DIM : (kv_head + 1) * HEAD_DIM] = dkey[span]
            ref[step, :, WIDTH_K + kv_head * HEAD_DIM : WIDTH_K + (kv_head + 1) * HEAD_DIM] = dvalue[span]


def scatter_out(total, info_ref, chips, fsdp, kept, sent):
    block_rows = total.shape[0] // (2 * chips * fsdp)
    if block_rows % ROW_TILE:
        kept[0][...] = total[...].astype(BF16)
        return
    for (steps, bits), keep, send in zip(halves_of(chips, fsdp), kept, sent):
        for slot, item in enumerate(halving_order(bits)):
            for at, step in enumerate(steps):
                for other, ref in ((0, keep), (1, send)):
                    row = block_row(info_ref, chips, fsdp, step, other, item, 1) * block_rows
                    row = pl.multiple_of(row, block_rows)
                    ref[slot, at] = total[pl.ds(row, block_rows), :].astype(BF16)


def out_grad_kernel(chips, fsdp, info_ref, left_ref, right_ref, *refs):
    halves = (len(refs) - 1) // 2
    kept, sent, total = refs[: max(halves, 1)], refs[halves : 2 * halves], refs[-1]
    total[...] = dot_nn(left_ref[...].T, right_ref[...])
    scatter_out(total, info_ref, chips, fsdp, kept, sent)


def projected_back_kernel(
    chips, fsdp, bias_width, came, info_ref, dq_ref, mine_ref, swapped_ref, cos_ref, sin_ref, unit_ref, *refs
):
    arrived = refs[:came]
    gp_ref, *refs = refs[came:]
    halves = (len(refs) - 1) // 2
    kept, sent, total = refs[: max(halves, 1)], refs[halves : 2 * halves], refs[-1]
    width = unit_ref.shape[1]
    block_rows = width // (2 * chips * fsdp)
    kv = mine_ref[...].astype(F32) + swapped_ref[...].astype(F32)
    for ref in arrived:
        kv = kv + ref[...].astype(F32)
    cosine, sine = cos_ref[...], sin_ref[...]
    for tile in range(QKV // LANES):
        at = tile * LANES
        head = dq_ref[:, at : at + LANES] if at < WIDTH_Q else kv[:, at - WIDTH_Q : at - WIDTH_Q + LANES]
        if at < WIDTH_Q + WIDTH_K:
            head = head * cosine - pltpu.roll(head, HEAD_DIM // 2, 1) * sine
        gp_ref[:, at : at + LANES] = head.astype(BF16)
    turned = unit_ref[...].T
    for at in range(0, QKV, 512):
        total[:, at : at + 512] = dot_nn(turned, gp_ref[:, at : at + 512])
    total[:, QKV:] = jnp.zeros((width, LANES), F32)
    each = LANES // bias_width
    for tile in range(QKV // LANES):
        sums = jnp.sum(gp_ref[:, tile * LANES : (tile + 1) * LANES].astype(F32), axis=0, keepdims=True)
        for member in range(each):
            block = (tile * each + member) * block_rows
            total[block : block + 8, QKV:] = jnp.broadcast_to(sums, (8, LANES))
    scatter_out(total, info_ref, chips, fsdp, kept, sent)


def input_back_kernel(plan, chips, fsdp, count, info_ref, gp_ref, tokens_ref, middle_ref, *refs):
    pieces = refs[:count]
    out_ref, whole, sems = refs[count:]
    width = tokens_ref.shape[1]
    rows = width // (2 * chips * fsdp)
    copies = copies_of(plan, info_ref, pieces, whole, sems, rows, (0, QKV), chips, fsdp)
    for copy in copies:
        copy.start()
    values = tokens_ref[...].astype(F32)
    rms = normalised(values)
    for copy in copies:
        copy.wait()
    unit_grad = dot_nt(gp_ref[...], whole[...])
    out_ref[...] = (
        middle_ref[...]
        + rms * unit_grad
        - values * (rms * rms * rms) * jnp.mean(unit_grad * values, axis=-1, keepdims=True)
    )


def call(kernel, outs, ins, any_from=None, any_to=None, scratch=(), estimate=None, name=None):
    specs = [SMEM_SPEC] + [VMEM_SPEC] * (len(ins) - 1)
    if any_from is not None:
        for index in range(any_from, any_to):
            specs[index] = ANY_SPEC
    many = isinstance(outs, (list, tuple))
    return pl.pallas_call(
        kernel,
        out_shape=outs,
        in_specs=specs,
        out_specs=[VMEM_SPEC] * len(outs) if many else VMEM_SPEC,
        scratch_shapes=list(scratch),
        compiler_params=params(),
        cost_estimate=estimate,
        name=name,
    )(*ins)


def shards(
    tokens,
    segments,
    positions,
    norm1_gain,
    qkv_weight,
    qkv_bias,
    out_weight,
    norm2_gain,
    gate_up_weight,
    down_weight,
    cotangent,
):
    inputs = tokens[0]
    grad_out = cotangent[0]
    rows, width = inputs.shape
    ctx = lax.axis_size("ctx")
    fsdp = lax.axis_size("fsdp")
    chips = ctx // 2
    my_ctx = lax.axis_index("ctx")
    my_fsdp = lax.axis_index("fsdp")
    info = jnp.stack([my_ctx, my_fsdp]).astype(jnp.int32)
    weight_rows = qkv_weight.shape[0]
    bias_width = qkv_bias.shape[0]
    own = gate_up_weight.shape[1] // 2 // ctx
    padded = -(-own // LANES) * LANES
    gain_one = norm1_gain.astype(F32)[:, None]
    gain_two = norm2_gain.astype(F32)[:, None]

    each = LANES // bias_width
    spot = (my_ctx * fsdp + my_fsdp) % each
    bias_row = jnp.where(
        jnp.arange(LANES, dtype=jnp.int32) // bias_width == spot, jnp.tile(qkv_bias, each), 0.0
    ).astype(BF16)
    bias_block = jnp.zeros((weight_rows, LANES), BF16).at[0].set(bias_row)
    packed = pl.pallas_call(
        pack_kernel,
        out_shape=struct((weight_rows, QKV + LANES + width), BF16),
        compiler_params=params(),
        name="pack",
    )(qkv_weight, bias_block, out_weight, gain_one)
    pieces, plan = gather_blocks(packed, chips, fsdp)

    split = call(
        functools.partial(split_kernel, chips, own, padded),
        struct((2, chips, weight_rows, 2 * padded), BF16),
        [info, gate_up_weight, gain_two],
        name="split",
    )
    w_down = lax.all_gather(down_weight, "fsdp", axis=0, tiled=True)
    arrived = [
        split[other, step] if (other, step) == (0, 0) else send_to(split[other, step], step, other)
        for other in range(2)
        for step in range(chips)
    ]
    aligned = weight_rows % ROW_TILE == 0
    arrived = jnp.stack(arrived)
    numbers = jnp.arange(ctx, dtype=jnp.int32)
    came_from = (numbers + my_ctx) % 2 * chips + (my_ctx // 2 - numbers // 2 + chips) % chips
    if not aligned:
        arrived = picked(arrived, came_from, 0)
    w_wide = lax.all_gather(arrived, "fsdp", axis=0, tiled=False)
    if not aligned:
        w_wide = w_wide.transpose(1, 0, 2, 3).reshape(width, 2 * padded)

    cot_mine = [grad_out]
    for step in range(1, chips):
        cot_mine.append(shift_chip(grad_out, step))
    cot_other = [swap_core(item) for item in cot_mine]

    steps_half = jnp.arange(0, HEAD_DIM, 2).astype(F32)
    inverse = 10000.0 ** (-steps_half / HEAD_DIM)
    turns = positions[0].astype(F32)[:, None] * inverse[None, :]
    cosine = jnp.tile(jnp.cos(turns), (1, 2))
    sine = jnp.concatenate([-jnp.sin(turns), jnp.sin(turns)], axis=-1)
    places = positions[0][:, None]
    count = len(pieces)
    unit_one, queries, own_kv = call(
        functools.partial(project_kernel, plan, chips, fsdp, bias_width, count),
        [struct((rows, width), BF16), struct((rows, WIDTH_Q), BF16), struct((rows, 2 * WIDTH_K), BF16)],
        [info, inputs, cosine, sine] + pieces,
        4,
        4 + count,
        [pltpu.VMEM((width, QKV + LANES), BF16), pltpu.SemaphoreType.DMA((len(plan or [0]),))],
        cost(2 * rows * width * QKV, 2 * width * QKV),
        "project",
    )
    reach = -(-chips // 2)
    kv_blocks, sources = [], []
    for step in range(reach + 1):
        block = own_kv if step == 0 else shift_open(own_kv, step)
        kv_blocks += [block, swap_core(block)]
        sources += [(step, 0), (step, 1)]
    span = len(sources) * rows
    context, middle, unit_two = call(
        functools.partial(attend_kernel, plan, chips, fsdp, count, sources),
        [struct((rows, width), BF16), struct((rows, width), F32), struct((rows, width), BF16)],
        [info, places, queries, inputs] + kv_blocks + pieces,
        4 + len(sources),
        4 + len(sources) + count,
        [pltpu.VMEM((width, width), BF16), pltpu.SemaphoreType.DMA((len(plan or [0]),))],
        cost(4 * rows * span * WIDTH_Q + 2 * rows * width * width, 2 * width * width, rows * span * Q_HEADS),
        "attend",
    )

    units_mine = [unit_two]
    for step in range(1, chips):
        units_mine.append(shift_chip(units_mine[-1], 1))
    units_other = [swap_core(item) for item in units_mine]
    fed = []
    for step in range(chips):
        fed.append(
            call(
                functools.partial(feed_kernel, chips, fsdp, own, padded),
                [struct((rows, width), BF16)] * 4
                + [struct((2 * rows, padded), BF16), struct((2 * rows, 2 * padded), BF16)],
                [info, units_mine[step], units_other[step], cot_mine[step], cot_other[step], w_wide, w_down],
                5,
                7,
                [
                    pltpu.VMEM((width, 2 * padded), BF16),
                    pltpu.VMEM((padded, width), BF16),
                    pltpu.VMEM((2 * rows, width), F32),
                    pltpu.VMEM((2 * rows, width), F32),
                    pltpu.SemaphoreType.DMA((ctx * fsdp + 1,)),
                ],
                cost(2 * 6 * 2 * rows * width * padded, 6 * width * padded),
                "feed",
            )
        )

    def ring(parts):
        sums = [mine + swap_core(other) for mine, other in parts]
        moving = None
        for step in range(1, chips):
            moving = shift_chip(sums[step] if moving is None else sums[step] + moving, 1)
        return sums[0], moving

    own_units, came_units = ring([(item[0], item[1]) for item in fed])

    n_block = 384 if (2 * padded) % 384 == 0 else LANES
    all_units = [item for pair in zip(units_mine, units_other) for item in pair]
    wide_grad = pl.pallas_call(
        functools.partial(wide_grad_kernel, chips, fsdp, ctx),
        out_shape=struct((fsdp, ctx, weight_rows, 2 * padded) if aligned else (width, 2 * padded), BF16),
        grid=(2 * padded // n_block,),
        in_specs=[SMEM_SPEC]
        + [pl.BlockSpec((rows, width), lambda i: (0, 0))] * ctx
        + [pl.BlockSpec((2 * rows, n_block), lambda i: (0, i))] * chips,
        out_specs=pl.BlockSpec((fsdp, ctx, weight_rows, n_block), lambda i: (0, 0, 0, i))
        if aligned
        else pl.BlockSpec((width, n_block), lambda i: (0, i)),
        scratch_shapes=[pltpu.VMEM((width, ctx * rows), BF16), pltpu.VMEM((width, n_block), F32)],
        compiler_params=params(),
        cost_estimate=cost(4 * ctx * rows * width * padded, 8 * width * padded),
        name="wide_grad",
    )(info, *all_units, *[item[5] for item in fed])
    d_block = 512
    all_cots = [item for pair in zip(cot_mine, cot_other) for item in pair]
    down_grad = pl.pallas_call(
        functools.partial(down_grad_kernel, own, chips),
        out_shape=struct((own, width), BF16),
        grid=(width // d_block,),
        in_specs=[pl.BlockSpec((2 * rows, padded), lambda i: (0, 0))] * chips
        + [pl.BlockSpec((rows, d_block), lambda i: (0, i))] * ctx,
        out_specs=pl.BlockSpec((own, d_block), lambda i: (0, i)),
        scratch_shapes=[pltpu.VMEM((padded, ctx * rows), BF16)],
        compiler_params=params(),
        cost_estimate=cost(2 * ctx * rows * width * padded, 4 * width * padded),
        name="down_grad",
    )(*[item[4] for item in fed], *all_cots)
    down_grad = lax.psum_scatter(down_grad, "fsdp", scatter_dimension=0, tiled=True).astype(F32)
    if not aligned:
        slots = jnp.arange(ctx, dtype=jnp.int32)
        goes_to = 2 * ((my_ctx // 2 + slots % chips) % chips) + (my_ctx + slots // chips) % 2
        wide_grad = wide_grad.reshape(ctx, fsdp, weight_rows, 2 * padded).transpose(1, 0, 2, 3)
        wide_grad = picked(wide_grad, goes_to, 1)
    wide_grad = lax.psum_scatter(
        wide_grad.reshape(fsdp * ctx * weight_rows, 2 * padded), "fsdp", scatter_dimension=0, tiled=True
    ).reshape(ctx, weight_rows, 2 * padded)
    back = [
        wide_grad[other * chips + step]
        if (other, step) == (0, 0)
        else send_to(wide_grad[other * chips + step], step, other)
        for other in range(2)
        for step in range(chips)
    ]
    gate_up_grad, norm2_grad = call(
        functools.partial(join_kernel, chips, own, padded),
        [struct(gate_up_weight.shape, F32), struct((weight_rows, 1), F32)],
        [info, jnp.stack(back), gate_up_weight, gain_two],
        name="join",
    )
    own_branch, came_branch = ring([(item[2], item[3]) for item in fed])
    result = (middle + own_branch.astype(F32) + came_branch.astype(F32)).astype(BF16)

    grad_middle, grad_attention, grad_queries, kv_mine, kv_other = call(
        functools.partial(middle_back_kernel, plan, chips, fsdp, count, sources),
        [
            struct((rows, width), F32),
            struct((rows, width), BF16),
            struct((rows, WIDTH_Q), F32),
            struct((reach + 1, rows, 2 * WIDTH_K), BF16),
            struct((reach + 1, rows, 2 * WIDTH_K), BF16),
        ],
        [info, places, queries, own_units, came_units, middle, grad_out] + kv_blocks + pieces,
        7 + len(sources),
        7 + len(sources) + count,
        [pltpu.VMEM((width, width), BF16), pltpu.SemaphoreType.DMA((len(plan or [0]),))],
        cost(10 * rows * span * WIDTH_Q + 2 * rows * width * width, 2 * width * width, rows * span * Q_HEADS),
        "middle_back",
    )
    halves = halves_of(chips, fsdp)
    kept_count = len(halves) if aligned else 1

    def block_shapes(columns):
        if not aligned:
            return [struct((width, columns), BF16)]
        return 2 * [struct((fsdp, len(steps), weight_rows, columns), BF16) for steps, _ in halves]

    outs = call(
        functools.partial(out_grad_kernel, chips, fsdp),
        block_shapes(width),
        [info, grad_attention, context],
        scratch=[pltpu.VMEM((width, width), F32)],
        estimate=cost(2 * rows * width * width, 2 * width * width),
        name="out_grad",
    )
    out_grad = reduce_blocks(outs[:kept_count], outs[kept_count:], chips, fsdp)

    swapped = swap_core(kv_other)
    came = []
    for step in range(1, reach + 1):
        came.append(shift_open(kv_mine[step] + swapped[step], -step))
    outs = call(
        functools.partial(projected_back_kernel, chips, fsdp, bias_width, reach),
        [struct((rows, QKV), BF16)] + block_shapes(QKV + LANES),
        [info, grad_queries, kv_mine[0], swapped[0], cosine, sine, unit_one] + came,
        scratch=[pltpu.VMEM((width, QKV + LANES), F32)],
        estimate=cost(2 * rows * width * QKV, 2 * width * QKV),
        name="projected_back",
    )
    grad_projected = outs[0]
    qkv_sum = reduce_blocks(outs[1 : 1 + kept_count], outs[1 + kept_count :], chips, fsdp)
    bias_row = lax.dynamic_slice_in_dim(qkv_sum[0], QKV + spot * bias_width, bias_width)
    qkv_sum = qkv_sum[:, :QKV]
    input_grad = call(
        functools.partial(input_back_kernel, plan, chips, fsdp, count),
        struct((rows, width), F32),
        [info, grad_projected, inputs, grad_middle] + pieces,
        4,
        4 + count,
        [pltpu.VMEM((width, QKV), BF16), pltpu.SemaphoreType.DMA((len(plan or [0]),))],
        cost(2 * rows * width * QKV, 2 * width * QKV),
        "input_back",
    )
    return (
        result[None],
        input_grad[None],
        jnp.sum(qkv_sum * qkv_weight.astype(F32), axis=1),
        qkv_sum * gain_one,
        bias_row,
        out_grad,
        norm2_grad[:, 0],
        gate_up_grad,
        down_grad,
    )


def solution(mesh):
    rows = P(BOTH, None)
    token = P("fsdp", "ctx", None)
    flat = P(BOTH)
    return jax.shard_map(
        shards,
        mesh=mesh,
        in_specs=(token, P("fsdp", "ctx"), P("fsdp", "ctx"), flat, rows, flat, rows, flat, rows, rows, token),
        out_specs=(token, token, flat, rows, flat, rows, flat, rows, rows),
        check_vma=False,
    )
```

```python
import functools

import jax
import jax.numpy as jnp
from jax import lax
from jax.experimental import pallas as pl
from jax.experimental.pallas import tpu as pltpu
from jax.sharding import PartitionSpec as P

Q_HEADS = 12
KV_HEADS = 2
HEAD_DIM = 128
GROUP = Q_HEADS // KV_HEADS
WIDTH_Q = Q_HEADS * HEAD_DIM
WIDTH_K = KV_HEADS * HEAD_DIM
QKV = WIDTH_Q + 2 * WIDTH_K
LANES = 128
ROW_TILE = 16
EPSILON = 1e-06
SCALE = HEAD_DIM ** (-0.5)
BF16 = jnp.bfloat16
F32 = jnp.float32
VMEM_LIMIT = 56 * 1024 * 1024
BOTH = ("ctx", "fsdp")

SMEM_SPEC = pl.BlockSpec(memory_space=pltpu.SMEM)
VMEM_SPEC = pl.BlockSpec(memory_space=pltpu.VMEM)
ANY_SPEC = pl.BlockSpec(memory_space=pl.ANY)


def dot_nn(left, right):
    return lax.dot_general(left, right, (((1,), (0,)), ((), ())), preferred_element_type=F32)


def dot_tn(left, right):
    return lax.dot_general(left, right, (((0,), (0,)), ((), ())), preferred_element_type=F32)


def dot_nt(left, right):
    return lax.dot_general(left, right, (((1,), (1,)), ((), ())), preferred_element_type=F32)


def params():
    return pltpu.CompilerParams(vmem_limit_bytes=VMEM_LIMIT)


def cost(flops, nbytes, exps=0):
    return pl.CostEstimate(flops=1, bytes_accessed=1, transcendentals=0)


def struct(shape, dtype):
    return jax.ShapeDtypeStruct(shape, dtype)


def swap_core(value):
    count = lax.axis_size("ctx")
    return lax.ppermute(value, "ctx", [(i, i ^ 1) for i in range(count)])


def shift_chip(value, steps):
    count = lax.axis_size("ctx")
    return lax.ppermute(value, "ctx", [(i, (i + 2 * steps) % count) for i in range(count)])


def shift_open(value, steps):
    count = lax.axis_size("ctx")
    pairs = [(i, i + 2 * steps) for i in range(count) if 0 <= i + 2 * steps < count]
    return lax.ppermute(value, "ctx", pairs)


def swap_fsdp(value, bit):
    count = lax.axis_size("fsdp")
    return lax.ppermute(value, "fsdp", [(i, i ^ bit) for i in range(count)])


def after(value, *others):
    return lax.optimization_barrier((value,) + others)[0]


def is_aligned(rows, fsdp):
    return rows % ROW_TILE == 0 and fsdp == 4


def bits_of(count):
    return [1 << k for k in range(count.bit_length() - 1)]


def halving_order(bits):
    if not bits:
        return [0]
    rest = halving_order(bits[1:])
    return [bits[0] ^ item for item in rest] + rest


def halves_of(chips, fsdp):
    bits = bits_of(fsdp)
    near = [step for step in range(chips) if step in (0, 1)]
    if chips > 2:
        far = [step for step in range(chips) if step not in near]
        return [(near, bits), (far, bits[::-1])]
    return [(near, bits)]


def spread(array, bits, waits=()):
    held = {0: array}
    for bit in bits:
        for item in list(held):
            held[item ^ bit] = swap_fsdp(held[item], bit)
    return held


def gather_head(packed, down, split, tables, chips):
    half = down.shape[1] // 2
    first, second = 1, 2
    left, right = after(down[:, :half], packed), after(down[:, half:], packed)
    moved = {0: packed, 1: shift_chip(packed, 1)}
    lefts, rights = {0: left, first: swap_fsdp(left, first)}, {0: right, second: swap_fsdp(right, second)}
    if chips > 2:
        moved[chips - 1] = shift_chip(packed, -1)
    lefts[second], rights[first] = swap_fsdp(left, second), swap_fsdp(right, first)
    done = [lefts[first], lefts[second], rights[first], rights[second], split] + list(moved.values())[1:]
    for step in range(2, chips - 1):
        moved[step] = shift_chip(after(moved[step - 1], *done), 1)
    lefts[3] = swap_fsdp(after(lefts[first], *done), second)
    rights[3] = swap_fsdp(after(rights[second], *done), first)
    done = [lefts[3], rights[3]] + [moved[step] for step in range(2, chips - 1)] + tables
    groups = [
        (steps, bits)
        for steps, bits in (
            ([step for step in range(chips) if step < 2], (first, second)),
            ([step for step in range(chips) if step >= 2], (second, first)),
        )
        if steps
    ]
    arrays, plan, held = [], [], []
    for steps, bits in groups:
        own = after(jnp.concatenate([moved[step] for step in steps], axis=0), *done)
        held.append({0: own, bits[0]: swap_fsdp(own, bits[0]), bits[1]: swap_fsdp(own, bits[1])})
    wide_part = lax.all_to_all(after(split, *done), "ctx", 0, 0)
    middle = [group[item] for group in held for item in (first, second)] + [wide_part]
    for group, (steps, bits) in zip(held, groups):
        group[3] = swap_fsdp(after(group[bits[0]], *middle), bits[1])
        for item, array in group.items():
            for other, version in ((0, array), (1, swap_core(array))):
                for block, step in enumerate(steps):
                    plan.append((len(arrays), block, step, other, item))
                arrays.append(version)
    downs = [lefts[item] for item in range(4)] + [rights[item] for item in range(4)]
    return arrays, plan, downs, wide_part, [wide_part] + [group[3] for group in held]


def reduce_chips(held, chips, fsdp):
    total = None
    for (steps, _), part_of in zip(halves_of(chips, fsdp), held):
        for at, step in enumerate(steps):
            part = part_of[at] if step == 0 else shift_chip(part_of[at], step)
            part = part.astype(F32)
            total = part if total is None else total + part
    return total


def block_row(info_ref, chips, fsdp, step, other, item, away=-1):
    chip = info_ref[0] // 2
    core = info_ref[0] % 2
    chip = (chip + away * step + chips) % chips
    core = 1 - core if other else core
    return (2 * chip + core) * fsdp + jnp.bitwise_xor(info_ref[1], item)


def copies_of(plan, info_ref, pieces, whole, sems, rows, columns, chips, fsdp):
    if plan is None:
        source = pieces[0].at[:, pl.ds(columns[0], columns[1])]
        return [pltpu.make_async_copy(source, whole, sems.at[0])]
    copies = []
    for index, (array, block, step, other, item) in enumerate(plan):
        row = block_row(info_ref, chips, fsdp, step, other, item) * rows
        row = pl.multiple_of(row, rows)
        source = pieces[array].at[pl.ds(block * rows, rows), pl.ds(columns[0], columns[1])]
        copies.append(pltpu.make_async_copy(source, whole.at[pl.ds(row, rows)], sems.at[index]))
    return copies


def normalised(values):
    return lax.rsqrt(jnp.mean(values * values, axis=-1, keepdims=True) + EPSILON)


def pack_kernel(qkv_ref, bias_ref, out_ref, gain_ref, packed_ref):
    packed_ref[:, :QKV] = (qkv_ref[...].astype(F32) * gain_ref[...]).astype(BF16)
    packed_ref[:, QKV : QKV + LANES] = bias_ref[...]
    packed_ref[:, QKV + LANES :] = out_ref[...]


def split_kernel(own, weight_ref, gain_ref, split_ref):
    total = weight_ref.shape[1] // 2
    count, rows, padded = split_ref.shape
    padded = padded // 2
    filler = jnp.zeros((rows, padded - own), F32)
    for target in range(count):
        for part in range(2):
            start = part * total + target * own
            values = weight_ref[:, start : start + own].astype(F32) * gain_ref[...]
            if padded > own:
                values = jnp.concatenate([values, filler], axis=1)
            split_ref[target, :, part * padded : (part + 1) * padded] = values.astype(BF16)


def join_kernel(own, gate_ref, up_ref, weight_ref, gain_ref, grad_ref, norm_ref):
    total = weight_ref.shape[1] // 2
    rows = weight_ref.shape[0]
    sums = jnp.zeros((rows, 1), F32)
    for source in range(gate_ref.shape[0]):
        for part, ref in enumerate((gate_ref, up_ref)):
            values = ref[source].astype(F32)[:, :own]
            start = part * total + source * own
            grad_ref[:, start : start + own] = values * gain_ref[...]
            sums = sums + jnp.sum(
                values * weight_ref[:, start : start + own].astype(F32), axis=1, keepdims=True
            )
    norm_ref[...] = sums


def stack_kernel(fsdp, info_ref, *refs):
    pieces, out_ref, whole = refs[:-2], refs[-2], refs[-1]
    rows, columns = pieces[0].shape
    for half in range(2):
        for item in range(fsdp):
            row = pl.multiple_of(jnp.bitwise_xor(info_ref[1], item) * rows, 8)
            whole[pl.ds(row, rows), half * columns : (half + 1) * columns] = pieces[half * fsdp + item][...].astype(F32)
    out_ref[...] = whole[...].astype(BF16)


def project_kernel(plan, chips, fsdp, bias_width, count, info_ref, tokens_ref, cos_ref, sin_ref, *refs):
    pieces = refs[:count]
    unit_ref, q_ref, kv_ref, whole, sems = refs[count:]
    width = tokens_ref.shape[1]
    rows = width // (2 * chips * fsdp)
    copies = copies_of(plan, info_ref, pieces, whole, sems, rows, (0, QKV + LANES), chips, fsdp)
    for copy in copies:
        copy.start()
    values = tokens_ref[...].astype(F32)
    unit = (values * normalised(values)).astype(BF16)
    unit_ref[...] = unit
    for copy in copies:
        copy.wait()
    cosine, sine = cos_ref[...], sin_ref[...]
    each = LANES // bias_width
    for tile in range(QKV // LANES):
        at = tile * LANES
        bias = jnp.zeros((1, LANES), F32)
        for member in range(each):
            block = (tile * each + member) * rows
            first = block // ROW_TILE * ROW_TILE
            group = whole[first : first + ROW_TILE, QKV:].astype(F32)
            bias = bias + group[block - first : block - first + 1]
        head = dot_nn(unit, whole[:, at : at + LANES]) + bias
        if at < WIDTH_Q + WIDTH_K:
            head = head * cosine + pltpu.roll(head, HEAD_DIM // 2, 1) * sine
        if at < WIDTH_Q:
            q_ref[:, at : at + LANES] = head.astype(BF16)
        else:
            kv_ref[:, at - WIDTH_Q : at - WIDTH_Q + LANES] = head.astype(BF16)


def key_mask(info_ref, place_ref, rows, sources):
    own = info_ref[0] * rows + lax.broadcasted_iota(jnp.int32, (rows, rows), 0)
    begin = own - place_ref[...]
    masks = []
    for step, other in sources:
        block = info_ref[0] - 2 * step
        if other:
            block = jnp.bitwise_xor(info_ref[0], 1) - 2 * step
        keys = block * rows + lax.broadcasted_iota(jnp.int32, (rows, rows), 1)
        masks.append((keys <= own) & (keys >= begin) & (keys >= 0))
    return jnp.concatenate(masks, axis=1)


def head_part(kv_refs, column):
    return jnp.concatenate([ref[:, column : column + HEAD_DIM] for ref in kv_refs], axis=0)


def probabilities(query, keys, allowed):
    scores = dot_nt(query, keys) * SCALE
    scores = jnp.where(allowed, scores, -1e30)
    exps = jnp.exp(scores - jnp.max(scores, axis=1, keepdims=True))
    return exps * (1.0 / jnp.sum(exps, axis=1, keepdims=True))


def attend_kernel(plan, chips, fsdp, count, sources, info_ref, place_ref, q_ref, tokens_ref, *refs):
    kv_refs = refs[: len(sources)]
    refs = refs[len(sources) :]
    pieces = refs[:count]
    context_ref, middle_ref, unit_ref, whole, sems = refs[count:]
    rows, width = tokens_ref.shape
    block_rows = width // (2 * chips * fsdp)
    copies = copies_of(
        plan, info_ref, pieces, whole, sems, block_rows, (QKV + LANES, width), chips, fsdp
    )
    for copy in copies:
        copy.start()
    allowed = key_mask(info_ref, place_ref, rows, sources)
    for kv_head in range(KV_HEADS):
        keys = head_part(kv_refs, kv_head * HEAD_DIM)
        values = head_part(kv_refs, WIDTH_K + kv_head * HEAD_DIM)
        for member in range(GROUP):
            at = (kv_head * GROUP + member) * HEAD_DIM
            probs = probabilities(q_ref[:, at : at + HEAD_DIM], keys, allowed).astype(BF16)
            context_ref[:, at : at + HEAD_DIM] = dot_nn(probs, values).astype(BF16)
    for copy in copies:
        copy.wait()
    middle = tokens_ref[...].astype(F32) + dot_nt(context_ref[...], whole[...])
    middle_ref[...] = middle
    unit_ref[...] = (middle * normalised(middle)).astype(BF16)


def tokens_of(info_ref, step, chips, rows):
    chip = (info_ref[0] // 2 - step + chips) % chips
    return pl.ds(pl.multiple_of(chip * 2 * rows, 2 * rows), 2 * rows)


def feed_kernel(
    steps, first, plan, chips, fsdp, own, padded, count, info_ref, units_ref, cots_ref, *refs
):
    pieces, down_ref = refs[: 2 * count], refs[2 * count]
    refs = refs[2 * count + (1 if first else 2) :]
    branch_ref, mine_ref, other_ref, hidden_ref, grad_ref = refs[:5]
    x, c, gate_w, up_w, down, acc_units, acc_branch, branch, gate_sems, up_sems, sems = refs[5:]
    _, rows, width = mine_ref.shape
    block_rows = width // (2 * chips * fsdp)
    spans = [tokens_of(info_ref, step, chips, rows) for step in steps]
    places = [pl.ds(index * 2 * rows, 2 * rows) for index in range(len(steps))]

    def loads(parts, whole, part_sems):
        if plan is None:
            return [pltpu.make_async_copy(parts[0], whole, part_sems.at[0])]
        copies = []
        for index, (array, block, item) in enumerate(plan):
            row = (block * fsdp + jnp.bitwise_xor(info_ref[1], item)) * block_rows
            row = pl.multiple_of(row, block_rows)
            source = parts[array].at[block]
            copies.append(
                pltpu.make_async_copy(source, whole.at[pl.ds(row, block_rows)], part_sems.at[index])
            )
        return copies

    x_loads = [
        pltpu.make_async_copy(units_ref.at[span], x.at[place], sems.at[index])
        for index, (span, place) in enumerate(zip(spans, places))
    ]
    c_loads = [
        pltpu.make_async_copy(cots_ref.at[span], c.at[place], sems.at[len(steps) + index])
        for index, (span, place) in enumerate(zip(spans, places))
    ]
    c_loads.append(pltpu.make_async_copy(down_ref, down.at[pl.ds(0, own)], sems.at[2 * len(steps)]))
    gate_loads = loads(pieces[:count], gate_w, gate_sems)
    up_loads = loads(pieces[count:], up_w, up_sems)
    for copy in x_loads + gate_loads + up_loads + c_loads:
        copy.start()
    if padded > own:
        down[own:, :] = jnp.zeros((padded - own, width), BF16)
    block = 384 if padded % 384 == 0 else LANES
    for copy in x_loads + gate_loads:
        copy.wait()
    for at in range(0, padded, block):
        cols = slice(at, at + block)
        cols_up = slice(padded + at, padded + at + block)
        gate = dot_nn(x[...], gate_w[:, cols])
        if at == 0:
            for copy in up_loads:
                copy.wait()
        up = dot_nn(x[...], up_w[:, cols])
        if at == 0:
            for copy in c_loads:
                copy.wait()
        grad_hidden = dot_nt(c[...], down[cols, :])
        sig = 1.0 / (1.0 + jnp.exp(-gate))
        swished = gate * sig
        hidden = (swished * up).astype(BF16)
        grad_gate = (grad_hidden * up * sig * (1.0 + gate * (1.0 - sig))).astype(BF16)
        grad_up = (grad_hidden * swished).astype(BF16)
        hidden_ref[cols, :] = hidden.T
        grad_ref[:, cols] = grad_gate
        grad_ref[:, cols_up] = grad_up
        units = dot_nt(grad_gate, gate_w[:, cols]) + dot_nt(grad_up, up_w[:, cols])
        more = dot_nn(hidden, down[cols, :])
        if at == 0:
            acc_units[...] = units
            acc_branch[...] = more
        else:
            acc_units[...] += units
            acc_branch[...] += more
    branch[...] = acc_branch[...].astype(BF16)
    stores = [
        pltpu.make_async_copy(branch.at[place], branch_ref.at[span], sems.at[index])
        for index, (span, place) in enumerate(zip(spans, places))
    ]
    for copy in stores:
        copy.start()
    core = info_ref[0] % 2
    for index in range(len(steps)):
        start = index * 2 * rows
        mine = pl.ds(pl.multiple_of(start + core * rows, rows), rows)
        other = pl.ds(pl.multiple_of(start + (1 - core) * rows, rows), rows)
        mine_ref[index] = acc_units[mine, :].astype(BF16)
        other_ref[index] = acc_units[other, :].astype(BF16)
    for copy in stores:
        copy.wait()


def turn_kernel(steps, chips, rows, info_ref, units_ref, out_ref):
    for index, step in enumerate(steps):
        span = tokens_of(info_ref, step, chips, rows)
        out_ref[:, index * 2 * rows : (index + 1) * 2 * rows] = units_ref[span, :].T


def wide_grad_kernel(orders, info_ref, turned, *refs):
    outs = 1 if orders is None else 4
    grads, out_refs, total = refs[: -1 - outs], refs[-1 - outs : -1], refs[-1]
    total[...] = dot_nn(turned[...], jnp.concatenate([grad[...] for grad in grads], axis=0))
    each, count, block_rows, _ = out_refs[0].shape
    if orders is None:
        for slot in range(each):
            for block in range(count):
                row = (block * each + slot) * block_rows
                out_refs[0][slot, block] = total[row : row + block_rows, :].astype(BF16)
        return
    fsdp = 2 * each
    for half, items in enumerate(orders):
        for slot, item in enumerate(items):
            for block in range(count):
                row = ((half * count + block) * fsdp + jnp.bitwise_xor(info_ref[1], item)) * block_rows
                row = pl.multiple_of(row, block_rows)
                out_refs[2 * half + slot // each][slot % each, block] = total[pl.ds(row, block_rows), :].astype(BF16)


def down_grad_kernel(orders, steps, chips, rows, info_ref, cots_ref, *refs):
    outs = 1 if orders is None else 4
    hiddens, out_refs, total = refs[: -1 - outs], refs[-1 - outs : -1], refs[-1]
    own, half = total.shape
    turned = jnp.concatenate([hidden[:own, :] for hidden in hiddens], axis=1)
    cots = jnp.concatenate([cots_ref[tokens_of(info_ref, step, chips, rows), :] for step in steps], axis=0)
    for index in range(cots.shape[1] // half):
        total[...] = dot_nn(turned, cots[:, index * half : (index + 1) * half])
        if orders is None:
            out_refs[0][:, index * half : (index + 1) * half] = total[...].astype(BF16)
            continue
        each = len(orders[0]) // 2
        part = own // len(orders[0])
        for slot, item in enumerate(orders[index]):
            row = pl.multiple_of(jnp.bitwise_xor(info_ref[1], item) * part, 8)
            out_refs[2 * index + slot // each][slot % each] = total[pl.ds(row, part), :].astype(BF16)


def middle_back_kernel(
    plan, chips, fsdp, count, sources, info_ref, place_ref, q_ref, middle_ref, cot_ref, *refs
):
    unit_refs, refs = refs[:chips], refs[chips:]
    kv_refs = refs[: len(sources)]
    refs = refs[len(sources) :]
    pieces = refs[:count]
    grad_ref, att_ref, dq_ref, mine_ref, other_ref, whole, sems = refs[count:]
    rows, width = middle_ref.shape
    block_rows = width // (2 * chips * fsdp)
    copies = copies_of(
        plan, info_ref, pieces, whole, sems, block_rows, (QKV + LANES, width), chips, fsdp
    )
    for copy in copies:
        copy.start()
    units = unit_refs[0][...].astype(F32)
    for ref in unit_refs[1:]:
        units = units + ref[...].astype(F32)
    middle = middle_ref[...]
    rms = normalised(middle)
    grad_middle = (
        cot_ref[...].astype(F32)
        + rms * units
        - middle * (rms * rms * rms) * jnp.mean(units * middle, axis=-1, keepdims=True)
    )
    grad_ref[...] = grad_middle
    attention = grad_middle.astype(BF16)
    att_ref[...] = attention
    allowed = key_mask(info_ref, place_ref, rows, sources)
    for copy in copies:
        copy.wait()
    context_grad = dot_nn(attention, whole[...]).astype(BF16)
    for kv_head in range(KV_HEADS):
        keys = head_part(kv_refs, kv_head * HEAD_DIM)
        values = head_part(kv_refs, WIDTH_K + kv_head * HEAD_DIM)
        dkey = None
        dvalue = None
        for member in range(GROUP):
            at = (kv_head * GROUP + member) * HEAD_DIM
            query = q_ref[:, at : at + HEAD_DIM]
            grad = context_grad[:, at : at + HEAD_DIM]
            probs = probabilities(query, keys, allowed)
            dprobs = dot_nt(grad, values)
            offset = jnp.sum(probs * dprobs, axis=1, keepdims=True)
            dscores = (probs * (dprobs - offset)).astype(BF16)
            dq_ref[:, at : at + HEAD_DIM] = dot_nn(dscores, keys) * SCALE
            more_key = dot_tn(dscores, query)
            more_value = dot_tn(probs.astype(BF16), grad)
            dkey = more_key if dkey is None else dkey + more_key
            dvalue = more_value if dvalue is None else dvalue + more_value
        dkey = (dkey * SCALE).astype(BF16)
        dvalue = dvalue.astype(BF16)
        for index, (step, other) in enumerate(sources):
            ref = other_ref if other else mine_ref
            span = slice(index * rows, (index + 1) * rows)
            ref[step, :, kv_head * HEAD_DIM : (kv_head + 1) * HEAD_DIM] = dkey[span]
            ref[step, :, WIDTH_K + kv_head * HEAD_DIM : WIDTH_K + (kv_head + 1) * HEAD_DIM] = dvalue[span]


def scatter_out(total, info_ref, chips, fsdp, kept, sent):
    block_rows = total.shape[0] // (2 * chips * fsdp)
    if not is_aligned(block_rows, fsdp):
        kept[0][...] = total[...].astype(BF16)
        return
    for (steps, bits), keep, send in zip(halves_of(chips, fsdp), kept, sent):
        for slot, item in enumerate(halving_order(bits)):
            for at, step in enumerate(steps):
                for other, ref in ((0, keep), (1, send)):
                    row = block_row(info_ref, chips, fsdp, step, other, item, 1) * block_rows
                    row = pl.multiple_of(row, block_rows)
                    ref[slot, at] = total[pl.ds(row, block_rows), :].astype(BF16)


def out_grad_kernel(chips, fsdp, info_ref, left_ref, right_ref, *refs):
    halves = (len(refs) - 1) // 2
    kept, sent, total = refs[: max(halves, 1)], refs[halves : 2 * halves], refs[-1]
    total[...] = dot_nn(left_ref[...].T, right_ref[...])
    scatter_out(total, info_ref, chips, fsdp, kept, sent)


def projected_back_kernel(
    chips, fsdp, bias_width, came, info_ref, dq_ref, mine_ref, swapped_ref, cos_ref, sin_ref, unit_ref, *refs
):
    arrived = refs[:came]
    gp_ref, *refs = refs[came:]
    halves = (len(refs) - 1) // 2
    kept, sent, total = refs[: max(halves, 1)], refs[halves : 2 * halves], refs[-1]
    width = unit_ref.shape[1]
    block_rows = width // (2 * chips * fsdp)
    kv = mine_ref[...].astype(F32) + swapped_ref[...].astype(F32)
    for ref in arrived:
        kv = kv + ref[...].astype(F32)
    cosine, sine = cos_ref[...], sin_ref[...]
    for tile in range(QKV // LANES):
        at = tile * LANES
        head = dq_ref[:, at : at + LANES] if at < WIDTH_Q else kv[:, at - WIDTH_Q : at - WIDTH_Q + LANES]
        if at < WIDTH_Q + WIDTH_K:
            head = head * cosine - pltpu.roll(head, HEAD_DIM // 2, 1) * sine
        gp_ref[:, at : at + LANES] = head.astype(BF16)
    turned = unit_ref[...].T
    for at in range(0, QKV, 512):
        total[:, at : at + 512] = dot_nn(turned, gp_ref[:, at : at + 512])
    total[:, QKV:] = jnp.zeros((width, LANES), F32)
    each = LANES // bias_width
    for tile in range(QKV // LANES):
        sums = jnp.sum(gp_ref[:, tile * LANES : (tile + 1) * LANES].astype(F32), axis=0, keepdims=True)
        for member in range(each):
            block = (tile * each + member) * block_rows
            total[block : block + 8, QKV:] = jnp.broadcast_to(sums, (8, LANES))
    scatter_out(total, info_ref, chips, fsdp, kept, sent)


def input_back_kernel(plan, chips, fsdp, count, info_ref, gp_ref, tokens_ref, middle_ref, *refs):
    pieces = refs[:count]
    out_ref, whole, sems = refs[count:]
    width = tokens_ref.shape[1]
    rows = width // (2 * chips * fsdp)
    copies = copies_of(plan, info_ref, pieces, whole, sems, rows, (0, QKV), chips, fsdp)
    for copy in copies:
        copy.start()
    values = tokens_ref[...].astype(F32)
    rms = normalised(values)
    for copy in copies:
        copy.wait()
    unit_grad = dot_nt(gp_ref[...], whole[...])
    out_ref[...] = (
        middle_ref[...]
        + rms * unit_grad
        - values * (rms * rms * rms) * jnp.mean(unit_grad * values, axis=-1, keepdims=True)
    )


def call(kernel, outs, ins, any_from=None, any_to=None, scratch=(), estimate=None, name=None):
    specs = [SMEM_SPEC] + [VMEM_SPEC] * (len(ins) - 1)
    if any_from is not None:
        for index in range(any_from, any_to):
            specs[index] = ANY_SPEC
    many = isinstance(outs, (list, tuple))
    return pl.pallas_call(
        kernel,
        out_shape=outs,
        in_specs=specs,
        out_specs=[VMEM_SPEC] * len(outs) if many else VMEM_SPEC,
        scratch_shapes=list(scratch),
        compiler_params=params(),
        cost_estimate=estimate,
        name=name,
    )(*ins)


def shards(
    tokens,
    segments,
    positions,
    norm1_gain,
    qkv_weight,
    qkv_bias,
    out_weight,
    norm2_gain,
    gate_up_weight,
    down_weight,
    cotangent,
):
    inputs = tokens[0]
    grad_out = cotangent[0]
    rows, width = inputs.shape
    ctx = lax.axis_size("ctx")
    fsdp = lax.axis_size("fsdp")
    chips = ctx // 2
    my_ctx = lax.axis_index("ctx")
    my_fsdp = lax.axis_index("fsdp")
    info = jnp.stack([my_ctx, my_fsdp]).astype(jnp.int32)
    weight_rows = qkv_weight.shape[0]
    bias_width = qkv_bias.shape[0]
    own = gate_up_weight.shape[1] // 2 // ctx
    padded = -(-own // LANES) * LANES
    gain_one = norm1_gain.astype(F32)[:, None]
    gain_two = norm2_gain.astype(F32)[:, None]

    each = LANES // bias_width
    spot = (my_ctx * fsdp + my_fsdp) % each
    bias_row = jnp.where(
        jnp.arange(LANES, dtype=jnp.int32) // bias_width == spot, jnp.tile(qkv_bias, each), 0.0
    ).astype(BF16)
    bias_block = jnp.zeros((weight_rows, LANES), BF16).at[0].set(bias_row)
    packed = pl.pallas_call(
        pack_kernel,
        out_shape=struct((weight_rows, QKV + LANES + width), BF16),
        compiler_params=params(),
        name="pack",
    )(qkv_weight, bias_block, out_weight, gain_one)
    own_down = down_weight.shape[0]
    aligned = is_aligned(weight_rows, fsdp) and own_down % 8 == 0
    split = pl.pallas_call(
        functools.partial(split_kernel, own),
        out_shape=struct((ctx, weight_rows, 2 * padded), BF16),
        compiler_params=params(),
        name="split",
    )(gate_up_weight, after(gain_two, packed))
    bits = bits_of(fsdp)
    d_half = width // 2
    steps_half = jnp.arange(0, HEAD_DIM, 2).astype(F32)
    inverse = 10000.0 ** (-steps_half / HEAD_DIM)
    angles = positions[0].astype(F32)[:, None] * inverse[None, :]
    cosine = jnp.tile(jnp.cos(angles), (1, 2))
    sine = jnp.concatenate([-jnp.sin(angles), jnp.sin(angles)], axis=-1)
    places = positions[0][:, None]
    if aligned:
        pieces, plan, down_held, wide_part, last = gather_head(
            packed, down_weight, split, [cosine, sine, places], chips
        )
        w_down = call(
            functools.partial(stack_kernel, fsdp),
            struct((own, width), BF16),
            [info] + down_held,
            scratch=[pltpu.VMEM((own, width), F32)],
            estimate=cost(0, 0),
            name="stack",
        )
    else:
        pieces, plan, last = [lax.all_gather(packed, BOTH, axis=0, tiled=True)], None, []
        wide_part = lax.all_to_all(split, "ctx", 0, 0)
        w_down = lax.all_gather(down_weight, "fsdp", axis=0, tiled=True)
    gate_part, up_part = wide_part[:, :, :padded], wide_part[:, :, padded:]
    if aligned:
        gate_held, up_held = spread(gate_part, bits), spread(up_part, bits[::-1])
        items = sorted(gate_held)
        near_wide = [gate_held[bits[0]], up_held[bits[-1]]]
        wide_plan = [(index, block, item) for index, item in enumerate(items) for block in range(ctx)]
        wide_pieces = [gate_held[item] for item in items] + [up_held[item] for item in items]
    else:
        wide_plan = None
        near_wide = []
        wide_pieces = [
            lax.all_gather(part, "fsdp", axis=1, tiled=False).reshape(width, padded)
            for part in (gate_part, up_part)
        ]
    wide_count = len(wide_pieces) // 2
    all_cots = lax.all_gather(after(grad_out, *last), "ctx", axis=0, tiled=True)

    count = len(pieces)
    unit_one, queries, own_kv = call(
        functools.partial(project_kernel, plan, chips, fsdp, bias_width, count),
        [struct((rows, width), BF16), struct((rows, WIDTH_Q), BF16), struct((rows, 2 * WIDTH_K), BF16)],
        [info, inputs, cosine, sine] + pieces,
        4,
        4 + count,
        [pltpu.VMEM((width, QKV + LANES), BF16), pltpu.SemaphoreType.DMA((len(plan or [0]),))],
        cost(2 * rows * width * QKV, 2 * width * QKV),
        "project",
    )
    reach = -(-chips // 2)
    kv_blocks, sources = [], []
    for step in range(reach + 1):
        block = own_kv if step == 0 else shift_open(own_kv, step)
        kv_blocks += [block, swap_core(block)]
        sources += [(step, 0), (step, 1)]
    span = len(sources) * rows
    context, middle, unit_two = call(
        functools.partial(attend_kernel, plan, chips, fsdp, count, sources),
        [struct((rows, width), BF16), struct((rows, width), F32), struct((rows, width), BF16)],
        [after(info, *near_wide), places, queries, inputs] + kv_blocks + pieces,
        4 + len(sources),
        4 + len(sources) + count,
        [pltpu.VMEM((width, width), BF16), pltpu.SemaphoreType.DMA((len(plan or [0]),))],
        cost(4 * rows * span * WIDTH_Q + 2 * rows * width * width, 2 * width * width, rows * span * Q_HEADS),
        "attend",
    )

    all_units = lax.all_gather(after(unit_two, all_cots), "ctx", axis=0, tiled=True)
    order = list(range(2, chips - 1)) + [1, chips - 1, 0] if chips > 2 else list(range(chips))[::-1]
    turned = call(
        functools.partial(turn_kernel, order, chips, rows),
        struct((width, ctx * rows), BF16),
        [after(info, w_down, *wide_pieces), all_units],
        estimate=cost(0, 4 * ctx * rows * width),
        name="turn",
    )
    half = len(order) // 2
    fed, unit_parts, branch, when = [], {}, [], turned
    for steps in (order[:half], order[half:]):
        tokens_now = 2 * rows * len(steps)
        plan_count = len(wide_plan or [0])
        operands = [after(info, when), all_units, all_cots] + wide_pieces + [w_down] + branch
        branch_now, mine, other, hidden, grads = pl.pallas_call(
            functools.partial(
                feed_kernel, steps, not branch, wide_plan, chips, fsdp, own, padded, wide_count
            ),
            out_shape=[
                struct((ctx * rows, width), BF16),
                struct((len(steps), rows, width), BF16),
                struct((len(steps), rows, width), BF16),
                struct((padded, tokens_now), BF16),
                struct((tokens_now, 2 * padded), BF16),
            ],
            in_specs=[SMEM_SPEC] + [ANY_SPEC] * (len(operands) - 1),
            out_specs=[ANY_SPEC] + [VMEM_SPEC] * 4,
            input_output_aliases={len(operands) - 1: 0} if branch else {},
            scratch_shapes=[
                pltpu.VMEM((tokens_now, width), BF16),
                pltpu.VMEM((tokens_now, width), BF16),
                pltpu.VMEM((width, padded), BF16),
                pltpu.VMEM((width, padded), BF16),
                pltpu.VMEM((padded, width), BF16),
                pltpu.VMEM((tokens_now, width), F32),
                pltpu.VMEM((tokens_now, width), F32),
                pltpu.VMEM((tokens_now, width), BF16),
                pltpu.SemaphoreType.DMA((plan_count,)),
                pltpu.SemaphoreType.DMA((plan_count,)),
                pltpu.SemaphoreType.DMA((2 * len(steps) + 1,)),
            ],
            compiler_params=params(),
            cost_estimate=cost(0, 0),
            name="feed",
        )(*operands)
        branch = [branch_now]
        fed.append((hidden, grads))
        early = list(unit_parts.values())
        swapped = swap_core(after(other, *early))
        for index, step in enumerate(steps):
            part = mine[index] + swapped[index]
            unit_parts[step] = shift_chip(part, -step) if step else part
        when = swapped
    n_block = 384 if padded % 384 == 0 else LANES

    def wide_grad(start, items, when):
        outs = 4 if items else 1
        shape = (fsdp // 2, chips, weight_rows, padded) if items else (fsdp, ctx, weight_rows, padded)
        return pl.pallas_call(
            functools.partial(wide_grad_kernel, items),
            out_shape=[struct(shape, BF16)] * outs,
            grid=(padded // n_block,),
            in_specs=[SMEM_SPEC, pl.BlockSpec((width, ctx * rows), lambda i: (0, 0))]
            + [
                pl.BlockSpec((grads.shape[0], n_block), lambda i: (0, start // n_block + i))
                for _, grads in fed
            ],
            out_specs=[pl.BlockSpec(shape[:3] + (n_block,), lambda i: (0, 0, 0, i))] * outs,
            scratch_shapes=[pltpu.VMEM((width, n_block), F32)],
            compiler_params=params(),
            cost_estimate=cost(2 * ctx * rows * width * padded, 4 * width * padded),
            name="wide_grad",
        )(when, turned, *[grads for _, grads in fed])

    turns = (bits, bits[::-1])
    wide_orders = [halving_order(items) for items in turns] if aligned else None
    gate_parts = wide_grad(0, wide_orders, after(info, *early))
    up_parts = wide_grad(padded, wide_orders, after(info, gate_parts[0]))

    def wide_first(parts, *waits):
        return [swap_fsdp(after(part, *waits), items[0]) for part, items in zip(parts[::2], turns)]

    def wide_second(parts, came, *waits):
        pairs = []
        for keep, more, items in zip(parts[1::2], came, turns):
            away = swap_fsdp(after(keep[0] + more[0], *waits), items[1])
            pairs.append((keep[1] + more[1], away))
        return pairs

    def wide_across(pairs, *waits):
        return lax.all_to_all(
            after(jnp.concatenate([mine + away for mine, away in pairs], axis=0), *waits), "ctx", 0, 0
        )

    gate_came = wide_first(gate_parts) if aligned else []
    up_came = wide_first(up_parts) if aligned else []

    grad_middle, grad_attention, grad_queries, kv_mine, kv_other = call(
        functools.partial(middle_back_kernel, plan, chips, fsdp, count, sources),
        [
            struct((rows, width), F32),
            struct((rows, width), BF16),
            struct((rows, WIDTH_Q), F32),
            struct((reach + 1, rows, 2 * WIDTH_K), BF16),
            struct((reach + 1, rows, 2 * WIDTH_K), BF16),
        ],
        [after(info, up_parts[0], *gate_came), places, queries, middle, grad_out]
        + [unit_parts[step] for step in range(chips)]
        + kv_blocks
        + pieces,
        5 + chips + len(sources),
        5 + chips + len(sources) + count,
        [pltpu.VMEM((width, width), BF16), pltpu.SemaphoreType.DMA((len(plan or [0]),))],
        cost(10 * rows * span * WIDTH_Q + 2 * rows * width * width, 2 * width * width, rows * span * Q_HEADS),
        "middle_back",
    )
    halves = halves_of(chips, fsdp)

    def block_shapes(columns):
        if not aligned:
            return [struct((width, columns), BF16)]
        return 2 * [struct((fsdp, len(steps), weight_rows, columns), BF16) for steps, _ in halves]

    out_parts = call(
        functools.partial(out_grad_kernel, chips, fsdp),
        block_shapes(width),
        [info, grad_attention, context],
        scratch=[pltpu.VMEM((width, width), F32)],
        estimate=cost(2 * rows * width * width, 2 * width * width),
        name="out_grad",
    )
    swapped = swap_core(after(kv_other, out_parts[0], *up_came))
    gate_pairs = wide_second(gate_parts, gate_came, out_parts[0], *up_came) if aligned else []
    if aligned:
        down_orders = [halving_order(bits), halving_order(bits[::-1])]
        down_shapes = [struct((fsdp // 2, own_down, d_half), BF16)] * 4
    else:
        down_orders = None
        down_shapes = [struct((own, width), BF16)]
    down_parts = call(
        functools.partial(down_grad_kernel, down_orders, order, chips, rows),
        down_shapes,
        [after(info, swapped), all_cots] + [hidden for hidden, _ in fed],
        scratch=[pltpu.VMEM((own, d_half), F32)],
        estimate=cost(2 * ctx * rows * width * padded, 4 * width * padded),
        name="down_grad",
    )
    came = []
    for step in range(1, reach + 1):
        came.append(shift_open(kv_mine[step] + swapped[step], -step))
    outs = call(
        functools.partial(projected_back_kernel, chips, fsdp, bias_width, reach),
        [struct((rows, QKV), BF16)] + block_shapes(QKV + LANES),
        [after(info, down_parts[0], *[away for _, away in gate_pairs]), grad_queries, kv_mine[0], swapped[0], cosine, sine, unit_one] + came,
        scratch=[pltpu.VMEM((width, QKV + LANES), F32)],
        estimate=cost(2 * rows * width * QKV, 2 * width * QKV),
        name="projected_back",
    )
    grad_projected, qkv_parts = outs[0], outs[1:]
    def back_to_input(waits):
        return call(
            functools.partial(input_back_kernel, plan, chips, fsdp, count),
            struct((rows, width), F32),
            [after(info, *waits), grad_projected, inputs, grad_middle] + pieces,
            4,
            4 + count,
            [pltpu.VMEM((width, QKV), BF16), pltpu.SemaphoreType.DMA((len(plan or [0]),))],
            cost(2 * rows * width * QKV, 2 * width * QKV),
            "input_back",
        )

    if aligned:
        sides = [items for _, items in halves]

        def swapped_of(parts, *waits):
            return [(keep, swap_core(after(send, *waits))) for keep, send in zip(parts[:2], parts[2:])]

        def first_exchange(pairs, *waits):
            half = fsdp // 2
            return [
                swap_fsdp(after(keep[:half] + got[:half], *waits), items[0])
                for (keep, got), items in zip(pairs, sides)
            ]

        def second_exchange(pairs, came_back):
            sums = []
            for (keep, got), more, items in zip(pairs, came_back, sides):
                away = swap_fsdp(keep[2] + got[2] + more[0], items[1])
                sums.append((keep[3] + got[3] + more[1], away))
            return [mine + away for mine, away in sums]

        up_pairs = wide_second(up_parts, up_came, *[away for _, away in gate_pairs])
        gate_back = wide_across(gate_pairs, grad_projected)
        qkv_pairs = swapped_of(qkv_parts)
        input_grad = back_to_input([])
        out_pairs = swapped_of(out_parts)
        out_came = first_exchange(out_pairs, *[away for _, away in gate_pairs])
        down_came = [
            swap_fsdp(after(part, *[away for _, away in gate_pairs]), items[0])
            for part, items in zip(down_parts[::2], (bits, bits[::-1]))
        ]
        qkv_came = first_exchange(qkv_pairs, input_grad, *[away for _, away in up_pairs], *out_came)
        up_back = wide_across(up_pairs, gate_back)
        qkv_far = second_exchange(qkv_pairs, [after(item, *down_came) for item in qkv_came])
        qkv_sum = reduce_chips(qkv_far, chips, fsdp)
        out_far = second_exchange(out_pairs, [after(item, *qkv_far) for item in out_came])
        out_grad = reduce_chips(out_far, chips, fsdp)
        down_away = [
            swap_fsdp(after(kept[0] + more[0], *qkv_far), items[1])
            for kept, more, items in zip(down_parts[1::2], down_came, (bits, bits[::-1]))
        ]
        down_grad = jnp.concatenate(
            [
                (kept[1] + more[1]).astype(F32) + away.astype(F32)
                for kept, more, away in zip(down_parts[1::2], down_came, down_away)
            ],
            axis=1,
        )
    else:

        def over(array, axes):
            return lax.psum_scatter(array, axes, scatter_dimension=0, tiled=True)

        qkv_sum, out_grad = (over(parts[0], BOTH).astype(F32) for parts in (qkv_parts, out_parts))
        down_grad = over(down_parts[0], "fsdp").astype(F32)
        gate_back, up_back = (
            lax.all_to_all(
                over(parts[0].reshape(-1, padded), "fsdp").reshape(ctx, weight_rows, padded), "ctx", 0, 0
            )
            for parts in (gate_parts, up_parts)
        )
        input_grad = back_to_input([])
    branch = lax.psum_scatter(after(branch[0], *early), "ctx", scatter_dimension=0, tiled=True)
    result = (middle + branch.astype(F32)).astype(BF16)
    gate_up_grad, norm2_grad = pl.pallas_call(
        functools.partial(join_kernel, own),
        out_shape=[struct(gate_up_weight.shape, F32), struct((weight_rows, 1), F32)],
        compiler_params=params(),
        name="join",
    )(gate_back, up_back, gate_up_weight, after(gain_two, input_grad))
    bias_row = lax.dynamic_slice_in_dim(qkv_sum[0], QKV + spot * bias_width, bias_width)
    qkv_sum = qkv_sum[:, :QKV]
    return (
        result[None],
        input_grad[None],
        jnp.sum(qkv_sum * qkv_weight.astype(F32), axis=1),
        qkv_sum * gain_one,
        bias_row,
        out_grad,
        norm2_grad[:, 0],
        gate_up_grad,
        down_grad,
    )


def solution(mesh):
    rows = P(BOTH, None)
    token = P("fsdp", "ctx", None)
    flat = P(BOTH)
    return jax.shard_map(
        shards,
        mesh=mesh,
        in_specs=(token, P("fsdp", "ctx"), P("fsdp", "ctx"), flat, rows, flat, rows, flat, rows, rows, token),
        out_specs=(token, token, flat, rows, flat, rows, flat, rows, rows),
        check_vma=False,
    )
```

```python
import functools

import jax
import jax.numpy as jnp
from jax import lax
from jax.experimental import pallas as pl
from jax.experimental.pallas import tpu as pltpu
from jax.sharding import PartitionSpec as P

Q_HEADS = 12
KV_HEADS = 2
HEAD_DIM = 128
GROUP = Q_HEADS // KV_HEADS
WIDTH_Q = Q_HEADS * HEAD_DIM
WIDTH_K = KV_HEADS * HEAD_DIM
QKV = WIDTH_Q + 2 * WIDTH_K
LANES = 128
ROW_TILE = 16
EPSILON = 1e-06
SCALE = HEAD_DIM ** (-0.5)
BF16 = jnp.bfloat16
F32 = jnp.float32
VMEM_LIMIT = 56 * 1024 * 1024
BOTH = ("ctx", "fsdp")

SMEM_SPEC = pl.BlockSpec(memory_space=pltpu.SMEM)
VMEM_SPEC = pl.BlockSpec(memory_space=pltpu.VMEM)
ANY_SPEC = pl.BlockSpec(memory_space=pl.ANY)


def dot_nn(left, right):
    return lax.dot_general(left, right, (((1,), (0,)), ((), ())), preferred_element_type=F32)


def dot_tn(left, right):
    return lax.dot_general(left, right, (((0,), (0,)), ((), ())), preferred_element_type=F32)


def dot_nt(left, right):
    return lax.dot_general(left, right, (((1,), (1,)), ((), ())), preferred_element_type=F32)


def params():
    return pltpu.CompilerParams(vmem_limit_bytes=VMEM_LIMIT)


def cost(flops, nbytes, exps=0):
    return pl.CostEstimate(flops=1, bytes_accessed=1, transcendentals=0)


def struct(shape, dtype):
    return jax.ShapeDtypeStruct(shape, dtype)


def swap_core(value):
    count = lax.axis_size("ctx")
    return lax.ppermute(value, "ctx", [(i, i ^ 1) for i in range(count)])


def shift_chip(value, steps):
    count = lax.axis_size("ctx")
    return lax.ppermute(value, "ctx", [(i, (i + 2 * steps) % count) for i in range(count)])


def shift_open(value, steps):
    count = lax.axis_size("ctx")
    pairs = [(i, i + 2 * steps) for i in range(count) if 0 <= i + 2 * steps < count]
    return lax.ppermute(value, "ctx", pairs)


def swap_fsdp(value, bit):
    count = lax.axis_size("fsdp")
    return lax.ppermute(value, "fsdp", [(i, i ^ bit) for i in range(count)])


def after(value, *others):
    return lax.optimization_barrier((value,) + others)[0]


def is_aligned(rows, fsdp):
    return rows % ROW_TILE == 0 and fsdp == 4


def bits_of(count):
    return [1 << k for k in range(count.bit_length() - 1)]


def halving_order(bits):
    if not bits:
        return [0]
    rest = halving_order(bits[1:])
    return [bits[0] ^ item for item in rest] + rest


def halves_of(chips, fsdp):
    bits = bits_of(fsdp)
    near = [step for step in range(chips) if step in (0, 1)]
    if chips > 2:
        far = [step for step in range(chips) if step not in near]
        return [(near, bits), (far, bits[::-1])]
    return [(near, bits)]


def spread(array, bits, waits=()):
    held = {0: array}
    for bit in bits:
        for item in list(held):
            held[item ^ bit] = swap_fsdp(held[item], bit)
    return held


def gather_head(packed, down, split, tables, chips):
    half = down.shape[1] // 2
    first, second = 1, 2
    left, right = after(down[:, :half], packed), after(down[:, half:], packed)
    moved = {0: packed, 1: shift_chip(packed, 1)}
    lefts, rights = {0: left, first: swap_fsdp(left, first)}, {0: right, second: swap_fsdp(right, second)}
    if chips > 2:
        moved[chips - 1] = shift_chip(packed, -1)
    lefts[second], rights[first] = swap_fsdp(left, second), swap_fsdp(right, first)
    done = [lefts[first], lefts[second], rights[first], rights[second], split] + list(moved.values())[1:]
    for step in range(2, chips - 1):
        moved[step] = shift_chip(after(moved[step - 1], *done), 1)
    lefts[3] = swap_fsdp(after(lefts[first], *done), second)
    rights[3] = swap_fsdp(after(rights[second], *done), first)
    done = [lefts[3], rights[3]] + [moved[step] for step in range(2, chips - 1)] + tables
    groups = [
        (steps, bits)
        for steps, bits in (
            ([step for step in range(chips) if step < 2], (first, second)),
            ([step for step in range(chips) if step >= 2], (second, first)),
        )
        if steps
    ]
    arrays, plan, held = [], [], []
    for steps, bits in groups:
        own = after(jnp.concatenate([moved[step] for step in steps], axis=0), *done)
        held.append({0: own, bits[0]: swap_fsdp(own, bits[0]), bits[1]: swap_fsdp(own, bits[1])})
    wide_part = lax.all_to_all(after(split, *done), "ctx", 0, 0)
    middle = [group[item] for group in held for item in (first, second)] + [wide_part]
    for group, (steps, bits) in zip(held, groups):
        group[3] = swap_fsdp(after(group[bits[0]], *middle), bits[1])
        for item, array in group.items():
            for other, version in ((0, array), (1, swap_core(array))):
                for block, step in enumerate(steps):
                    plan.append((len(arrays), block, step, other, item))
                arrays.append(version)
    downs = [lefts[item] for item in range(4)] + [rights[item] for item in range(4)]
    return arrays, plan, downs, wide_part, [wide_part] + [group[3] for group in held]


def reduce_chips(held, chips, fsdp):
    total = None
    for (steps, _), part_of in zip(halves_of(chips, fsdp), held):
        for at, step in enumerate(steps):
            part = part_of[at] if step == 0 else shift_chip(part_of[at], step)
            part = part.astype(F32)
            total = part if total is None else total + part
    return total


def block_row(info_ref, chips, fsdp, step, other, item, away=-1):
    chip = info_ref[0] // 2
    core = info_ref[0] % 2
    chip = (chip + away * step + chips) % chips
    core = 1 - core if other else core
    return (2 * chip + core) * fsdp + jnp.bitwise_xor(info_ref[1], item)


def copies_of(plan, info_ref, pieces, whole, sems, rows, columns, chips, fsdp):
    if plan is None:
        source = pieces[0].at[:, pl.ds(columns[0], columns[1])]
        return [pltpu.make_async_copy(source, whole, sems.at[0])]
    copies = []
    for index, (array, block, step, other, item) in enumerate(plan):
        row = block_row(info_ref, chips, fsdp, step, other, item) * rows
        row = pl.multiple_of(row, rows)
        source = pieces[array].at[pl.ds(block * rows, rows), pl.ds(columns[0], columns[1])]
        copies.append(pltpu.make_async_copy(source, whole.at[pl.ds(row, rows)], sems.at[index]))
    return copies


def normalised(values):
    return lax.rsqrt(jnp.mean(values * values, axis=-1, keepdims=True) + EPSILON)


def pack_kernel(qkv_ref, bias_ref, out_ref, gain_ref, packed_ref):
    packed_ref[:, :QKV] = (qkv_ref[...].astype(F32) * gain_ref[...]).astype(BF16)
    packed_ref[:, QKV : QKV + LANES] = bias_ref[...]
    packed_ref[:, QKV + LANES :] = out_ref[...]


def split_kernel(own, weight_ref, gain_ref, split_ref):
    total = weight_ref.shape[1] // 2
    count, rows, padded = split_ref.shape
    padded = padded // 2
    filler = jnp.zeros((rows, padded - own), F32)
    for target in range(count):
        for part in range(2):
            start = part * total + target * own
            values = weight_ref[:, start : start + own].astype(F32) * gain_ref[...]
            if padded > own:
                values = jnp.concatenate([values, filler], axis=1)
            split_ref[target, :, part * padded : (part + 1) * padded] = values.astype(BF16)


def join_kernel(own, gate_ref, up_ref, weight_ref, gain_ref, grad_ref, norm_ref):
    total = weight_ref.shape[1] // 2
    rows = weight_ref.shape[0]
    sums = jnp.zeros((rows, 1), F32)
    for source in range(gate_ref.shape[0]):
        for part, ref in enumerate((gate_ref, up_ref)):
            values = ref[source].astype(F32)[:, :own]
            start = part * total + source * own
            grad_ref[:, start : start + own] = values * gain_ref[...]
            sums = sums + jnp.sum(
                values * weight_ref[:, start : start + own].astype(F32), axis=1, keepdims=True
            )
    norm_ref[...] = sums


def stack_kernel(fsdp, info_ref, *refs):
    pieces, out_ref, whole = refs[:-2], refs[-2], refs[-1]
    rows, columns = pieces[0].shape
    for half in range(2):
        for item in range(fsdp):
            row = pl.multiple_of(jnp.bitwise_xor(info_ref[1], item) * rows, 8)
            whole[pl.ds(row, rows), half * columns : (half + 1) * columns] = pieces[half * fsdp + item][...].astype(F32)
    out_ref[...] = whole[...].astype(BF16)


def project_kernel(plan, chips, fsdp, bias_width, count, info_ref, tokens_ref, cos_ref, sin_ref, *refs):
    pieces = refs[:count]
    unit_ref, q_ref, kv_ref, whole, sems = refs[count:]
    width = tokens_ref.shape[1]
    rows = width // (2 * chips * fsdp)
    copies = copies_of(plan, info_ref, pieces, whole, sems, rows, (0, QKV + LANES), chips, fsdp)
    for copy in copies:
        copy.start()
    values = tokens_ref[...].astype(F32)
    unit = (values * normalised(values)).astype(BF16)
    unit_ref[...] = unit
    for copy in copies:
        copy.wait()
    cosine, sine = cos_ref[...], sin_ref[...]
    each = LANES // bias_width
    for tile in range(QKV // LANES):
        at = tile * LANES
        bias = jnp.zeros((1, LANES), F32)
        for member in range(each):
            block = (tile * each + member) * rows
            first = block // ROW_TILE * ROW_TILE
            group = whole[first : first + ROW_TILE, QKV:].astype(F32)
            bias = bias + group[block - first : block - first + 1]
        head = dot_nn(unit, whole[:, at : at + LANES]) + bias
        if at < WIDTH_Q + WIDTH_K:
            head = head * cosine + pltpu.roll(head, HEAD_DIM // 2, 1) * sine
        if at < WIDTH_Q:
            q_ref[:, at : at + LANES] = head.astype(BF16)
        else:
            kv_ref[:, at - WIDTH_Q : at - WIDTH_Q + LANES] = head.astype(BF16)


def key_mask(info_ref, place_ref, rows, sources):
    own = info_ref[0] * rows + lax.broadcasted_iota(jnp.int32, (rows, rows), 0)
    begin = own - place_ref[...]
    masks = []
    for step, other in sources:
        block = info_ref[0] - 2 * step
        if other:
            block = jnp.bitwise_xor(info_ref[0], 1) - 2 * step
        keys = block * rows + lax.broadcasted_iota(jnp.int32, (rows, rows), 1)
        masks.append((keys <= own) & (keys >= begin) & (keys >= 0))
    return jnp.concatenate(masks, axis=1)


def head_part(kv_refs, column):
    return jnp.concatenate([ref[:, column : column + HEAD_DIM] for ref in kv_refs], axis=0)


def probabilities(query, keys, allowed):
    scores = dot_nt(query, keys) * SCALE
    scores = jnp.where(allowed, scores, -1e30)
    exps = jnp.exp(scores - jnp.max(scores, axis=1, keepdims=True))
    return exps * (1.0 / jnp.sum(exps, axis=1, keepdims=True))


def attend_kernel(plan, chips, fsdp, count, sources, info_ref, place_ref, q_ref, tokens_ref, *refs):
    kv_refs = refs[: len(sources)]
    refs = refs[len(sources) :]
    pieces = refs[:count]
    context_ref, middle_ref, unit_ref, whole, sems = refs[count:]
    rows, width = tokens_ref.shape
    block_rows = width // (2 * chips * fsdp)
    copies = copies_of(
        plan, info_ref, pieces, whole, sems, block_rows, (QKV + LANES, width), chips, fsdp
    )
    for copy in copies:
        copy.start()
    allowed = key_mask(info_ref, place_ref, rows, sources)
    for kv_head in range(KV_HEADS):
        keys = head_part(kv_refs, kv_head * HEAD_DIM)
        values = head_part(kv_refs, WIDTH_K + kv_head * HEAD_DIM)
        for member in range(GROUP):
            at = (kv_head * GROUP + member) * HEAD_DIM
            probs = probabilities(q_ref[:, at : at + HEAD_DIM], keys, allowed).astype(BF16)
            context_ref[:, at : at + HEAD_DIM] = dot_nn(probs, values).astype(BF16)
    for copy in copies:
        copy.wait()
    middle = tokens_ref[...].astype(F32) + dot_nt(context_ref[...], whole[...])
    middle_ref[...] = middle
    unit_ref[...] = (middle * normalised(middle)).astype(BF16)


def tokens_of(info_ref, step, chips, rows):
    chip = (info_ref[0] // 2 - step + chips) % chips
    return pl.ds(pl.multiple_of(chip * 2 * rows, 2 * rows), 2 * rows)


def hidden_grad_kernel(steps, chips, rows, padded, info_ref, cots_ref, down_ref, out_ref):
    own = down_ref.shape[0]
    for index, step in enumerate(steps):
        part = dot_nt(cots_ref[tokens_of(info_ref, step, chips, rows), :], down_ref[...]).astype(BF16)
        out_ref[index * 2 * rows : (index + 1) * 2 * rows, :own] = part
        if padded > own:
            out_ref[index * 2 * rows : (index + 1) * 2 * rows, own:] = jnp.zeros((2 * rows, padded - own), BF16)


def branch_kernel(groups, chips, rows, info_ref, down_ref, *refs):
    hiddens, out_ref = refs[:-1], refs[-1]
    own = down_ref.shape[0]
    for steps, hidden in zip(groups, hiddens):
        for index, step in enumerate(steps):
            part = hidden[:own, index * 2 * rows : (index + 1) * 2 * rows]
            out_ref[tokens_of(info_ref, step, chips, rows), :] = dot_tn(part, down_ref[...]).astype(BF16)


def feed_kernel(steps, offset, plan, chips, fsdp, padded, count, info_ref, units_ref, c_ref, *refs):
    pieces, refs = refs[: 2 * count], refs[2 * count :]
    mine_ref, other_ref, hidden_ref, grad_ref = refs[:4]
    x, c, gate_w, up_w, acc_units, gate_sems, up_sems, sems = refs[4:]
    _, rows, width = mine_ref.shape
    block_rows = width // (2 * chips * fsdp)
    tokens = 2 * rows * len(steps)

    def loads(parts, whole, part_sems):
        if plan is None:
            return [pltpu.make_async_copy(parts[0], whole, part_sems.at[0])]
        copies = []
        for index, (array, block, item) in enumerate(plan):
            row = (block * fsdp + jnp.bitwise_xor(info_ref[1], item)) * block_rows
            row = pl.multiple_of(row, block_rows)
            source = parts[array].at[block]
            copies.append(
                pltpu.make_async_copy(source, whole.at[pl.ds(row, block_rows)], part_sems.at[index])
            )
        return copies

    x_loads = [
        pltpu.make_async_copy(
            units_ref.at[tokens_of(info_ref, step, chips, rows)],
            x.at[pl.ds(index * 2 * rows, 2 * rows)],
            sems.at[index],
        )
        for index, step in enumerate(steps)
    ]
    c_load = pltpu.make_async_copy(c_ref.at[pl.ds(offset, tokens)], c, sems.at[len(steps)])
    gate_loads = loads(pieces[:count], gate_w, gate_sems)
    up_loads = loads(pieces[count:], up_w, up_sems)
    for copy in x_loads + gate_loads + up_loads + [c_load]:
        copy.start()
    block = 384 if padded % 384 == 0 else LANES
    for copy in x_loads + gate_loads:
        copy.wait()
    for at in range(0, padded, block):
        cols = slice(at, at + block)
        cols_up = slice(padded + at, padded + at + block)
        gate = dot_nn(x[...], gate_w[:, cols])
        if at == 0:
            for copy in up_loads:
                copy.wait()
        up = dot_nn(x[...], up_w[:, cols])
        if at == 0:
            c_load.wait()
        grad_hidden = c[:, cols].astype(F32)
        sig = 1.0 / (1.0 + jnp.exp(-gate))
        swished = gate * sig
        hidden = (swished * up).astype(BF16)
        grad_gate = (grad_hidden * up * sig * (1.0 + gate * (1.0 - sig))).astype(BF16)
        grad_up = (grad_hidden * swished).astype(BF16)
        hidden_ref[cols, :] = hidden.T
        grad_ref[:, cols] = grad_gate
        grad_ref[:, cols_up] = grad_up
        units = dot_nt(grad_gate, gate_w[:, cols]) + dot_nt(grad_up, up_w[:, cols])
        if at == 0:
            acc_units[...] = units
        else:
            acc_units[...] += units
    core = info_ref[0] % 2
    for index in range(len(steps)):
        start = index * 2 * rows
        mine = pl.ds(pl.multiple_of(start + core * rows, rows), rows)
        other = pl.ds(pl.multiple_of(start + (1 - core) * rows, rows), rows)
        mine_ref[index] = acc_units[mine, :].astype(BF16)
        other_ref[index] = acc_units[other, :].astype(BF16)


def sum_kernel(plan, count, info_ref, *refs):
    for terms, out_ref in zip(plan, refs[count:]):
        total = None
        for number, index in terms:
            term = (refs[number][...] if index is None else refs[number][index]).astype(F32)
            total = term if total is None else total + term
        out_ref[...] = total.astype(out_ref.dtype)


def turn_kernel(steps, chips, rows, info_ref, units_ref, out_ref):
    for index, step in enumerate(steps):
        span = tokens_of(info_ref, step, chips, rows)
        out_ref[:, index * 2 * rows : (index + 1) * 2 * rows] = units_ref[span, :].T


def wide_grad_kernel(orders, info_ref, turned, *refs):
    outs = 1 if orders is None else 4
    grads, out_refs, total = refs[: -1 - outs], refs[-1 - outs : -1], refs[-1]
    total[...] = dot_nn(turned[...], jnp.concatenate([grad[...] for grad in grads], axis=0))
    each, count, block_rows, _ = out_refs[0].shape
    if orders is None:
        for slot in range(each):
            for block in range(count):
                row = (block * each + slot) * block_rows
                out_refs[0][slot, block] = total[row : row + block_rows, :].astype(BF16)
        return
    fsdp = 2 * each
    for half, items in enumerate(orders):
        for slot, item in enumerate(items):
            for block in range(count):
                row = ((half * count + block) * fsdp + jnp.bitwise_xor(info_ref[1], item)) * block_rows
                row = pl.multiple_of(row, block_rows)
                out_refs[2 * half + slot // each][slot % each, block] = total[pl.ds(row, block_rows), :].astype(BF16)


def down_grad_kernel(orders, steps, chips, rows, info_ref, cots_ref, *refs):
    outs = 1 if orders is None else 4
    hiddens, out_refs, total = refs[: -1 - outs], refs[-1 - outs : -1], refs[-1]
    own, half = total.shape
    turned = jnp.concatenate([hidden[:own, :] for hidden in hiddens], axis=1)
    cots = jnp.concatenate([cots_ref[tokens_of(info_ref, step, chips, rows), :] for step in steps], axis=0)
    for index in range(cots.shape[1] // half):
        total[...] = dot_nn(turned, cots[:, index * half : (index + 1) * half])
        if orders is None:
            out_refs[0][:, index * half : (index + 1) * half] = total[...].astype(BF16)
            continue
        each = len(orders[0]) // 2
        part = own // len(orders[0])
        for slot, item in enumerate(orders[index]):
            row = pl.multiple_of(jnp.bitwise_xor(info_ref[1], item) * part, 8)
            out_refs[2 * index + slot // each][slot % each] = total[pl.ds(row, part), :].astype(BF16)


def middle_back_kernel(
    plan, chips, fsdp, count, sources, info_ref, place_ref, q_ref, middle_ref, cot_ref, *refs
):
    unit_refs, refs = refs[:chips], refs[chips:]
    kv_refs = refs[: len(sources)]
    refs = refs[len(sources) :]
    pieces = refs[:count]
    grad_ref, att_ref, dq_ref, mine_ref, other_ref, whole, sems = refs[count:]
    rows, width = middle_ref.shape
    block_rows = width // (2 * chips * fsdp)
    copies = copies_of(
        plan, info_ref, pieces, whole, sems, block_rows, (QKV + LANES, width), chips, fsdp
    )
    for copy in copies:
        copy.start()
    units = unit_refs[0][...].astype(F32)
    for ref in unit_refs[1:]:
        units = units + ref[...].astype(F32)
    middle = middle_ref[...]
    rms = normalised(middle)
    grad_middle = (
        cot_ref[...].astype(F32)
        + rms * units
        - middle * (rms * rms * rms) * jnp.mean(units * middle, axis=-1, keepdims=True)
    )
    grad_ref[...] = grad_middle
    attention = grad_middle.astype(BF16)
    att_ref[...] = attention
    allowed = key_mask(info_ref, place_ref, rows, sources)
    for copy in copies:
        copy.wait()
    context_grad = dot_nn(attention, whole[...]).astype(BF16)
    for kv_head in range(KV_HEADS):
        keys = head_part(kv_refs, kv_head * HEAD_DIM)
        values = head_part(kv_refs, WIDTH_K + kv_head * HEAD_DIM)
        dkey = None
        dvalue = None
        for member in range(GROUP):
            at = (kv_head * GROUP + member) * HEAD_DIM
            query = q_ref[:, at : at + HEAD_DIM]
            grad = context_grad[:, at : at + HEAD_DIM]
            probs = probabilities(query, keys, allowed)
            dprobs = dot_nt(grad, values)
            offset = jnp.sum(probs * dprobs, axis=1, keepdims=True)
            dscores = (probs * (dprobs - offset)).astype(BF16)
            dq_ref[:, at : at + HEAD_DIM] = dot_nn(dscores, keys) * SCALE
            more_key = dot_tn(dscores, query)
            more_value = dot_tn(probs.astype(BF16), grad)
            dkey = more_key if dkey is None else dkey + more_key
            dvalue = more_value if dvalue is None else dvalue + more_value
        dkey = (dkey * SCALE).astype(BF16)
        dvalue = dvalue.astype(BF16)
        for index, (step, other) in enumerate(sources):
            ref = other_ref if other else mine_ref
            span = slice(index * rows, (index + 1) * rows)
            ref[step, :, kv_head * HEAD_DIM : (kv_head + 1) * HEAD_DIM] = dkey[span]
            ref[step, :, WIDTH_K + kv_head * HEAD_DIM : WIDTH_K + (kv_head + 1) * HEAD_DIM] = dvalue[span]


def scatter_out(total, info_ref, chips, fsdp, kept, sent):
    block_rows = total.shape[0] // (2 * chips * fsdp)
    if not is_aligned(block_rows, fsdp):
        kept[0][...] = total[...].astype(BF16)
        return
    for (steps, bits), keep, send in zip(halves_of(chips, fsdp), kept, sent):
        for slot, item in enumerate(halving_order(bits)):
            for at, step in enumerate(steps):
                for other, ref in ((0, keep), (1, send)):
                    row = block_row(info_ref, chips, fsdp, step, other, item, 1) * block_rows
                    row = pl.multiple_of(row, block_rows)
                    ref[slot, at] = total[pl.ds(row, block_rows), :].astype(BF16)


def out_grad_kernel(chips, fsdp, info_ref, left_ref, right_ref, *refs):
    halves = (len(refs) - 1) // 2
    kept, sent, total = refs[: max(halves, 1)], refs[halves : 2 * halves], refs[-1]
    total[...] = dot_nn(left_ref[...].T, right_ref[...])
    scatter_out(total, info_ref, chips, fsdp, kept, sent)


def projected_back_kernel(
    chips, fsdp, bias_width, came, info_ref, dq_ref, mine_ref, swapped_ref, cos_ref, sin_ref, unit_ref, *refs
):
    arrived = refs[:came]
    gp_ref, *refs = refs[came:]
    halves = (len(refs) - 1) // 2
    kept, sent, total = refs[: max(halves, 1)], refs[halves : 2 * halves], refs[-1]
    width = unit_ref.shape[1]
    block_rows = width // (2 * chips * fsdp)
    kv = mine_ref[...].astype(F32) + swapped_ref[...].astype(F32)
    for ref in arrived:
        kv = kv + ref[...].astype(F32)
    cosine, sine = cos_ref[...], sin_ref[...]
    for tile in range(QKV // LANES):
        at = tile * LANES
        head = dq_ref[:, at : at + LANES] if at < WIDTH_Q else kv[:, at - WIDTH_Q : at - WIDTH_Q + LANES]
        if at < WIDTH_Q + WIDTH_K:
            head = head * cosine - pltpu.roll(head, HEAD_DIM // 2, 1) * sine
        gp_ref[:, at : at + LANES] = head.astype(BF16)
    turned = unit_ref[...].T
    for at in range(0, QKV, 512):
        total[:, at : at + 512] = dot_nn(turned, gp_ref[:, at : at + 512])
    total[:, QKV:] = jnp.zeros((width, LANES), F32)
    each = LANES // bias_width
    for tile in range(QKV // LANES):
        sums = jnp.sum(gp_ref[:, tile * LANES : (tile + 1) * LANES].astype(F32), axis=0, keepdims=True)
        for member in range(each):
            block = (tile * each + member) * block_rows
            total[block : block + 8, QKV:] = jnp.broadcast_to(sums, (8, LANES))
    scatter_out(total, info_ref, chips, fsdp, kept, sent)


def input_back_kernel(plan, chips, fsdp, count, info_ref, gp_ref, tokens_ref, middle_ref, *refs):
    pieces = refs[:count]
    out_ref, whole, sems = refs[count:]
    width = tokens_ref.shape[1]
    rows = width // (2 * chips * fsdp)
    copies = copies_of(plan, info_ref, pieces, whole, sems, rows, (0, QKV), chips, fsdp)
    for copy in copies:
        copy.start()
    values = tokens_ref[...].astype(F32)
    rms = normalised(values)
    for copy in copies:
        copy.wait()
    unit_grad = dot_nt(gp_ref[...], whole[...])
    out_ref[...] = (
        middle_ref[...]
        + rms * unit_grad
        - values * (rms * rms * rms) * jnp.mean(unit_grad * values, axis=-1, keepdims=True)
    )


def call(kernel, outs, ins, any_from=None, any_to=None, scratch=(), estimate=None, name=None):
    specs = [SMEM_SPEC] + [VMEM_SPEC] * (len(ins) - 1)
    if any_from is not None:
        for index in range(any_from, any_to):
            specs[index] = ANY_SPEC
    many = isinstance(outs, (list, tuple))
    return pl.pallas_call(
        kernel,
        out_shape=outs,
        in_specs=specs,
        out_specs=[VMEM_SPEC] * len(outs) if many else VMEM_SPEC,
        scratch_shapes=list(scratch),
        compiler_params=params(),
        cost_estimate=estimate,
        name=name,
    )(*ins)


def sums(when, *outs):
    arrays, plan, shapes = [], [], []
    for terms in outs:
        row = []
        for array, index in terms:
            row.append((len(arrays), index))
            arrays.append(array)
        array, index = terms[0]
        shape = array.shape
        if isinstance(index, slice):
            shape = (len(range(*index.indices(shape[0]))),) + shape[1:]
        elif index is not None:
            shape = shape[1:]
        plan.append(row)
        shapes.append(struct(shape, BF16))
    return call(
        functools.partial(sum_kernel, plan, len(arrays)),
        shapes,
        [when] + arrays,
        estimate=cost(0, 0),
        name="sums",
    )


def shards(
    tokens,
    segments,
    positions,
    norm1_gain,
    qkv_weight,
    qkv_bias,
    out_weight,
    norm2_gain,
    gate_up_weight,
    down_weight,
    cotangent,
):
    inputs = tokens[0]
    grad_out = cotangent[0]
    rows, width = inputs.shape
    ctx = lax.axis_size("ctx")
    fsdp = lax.axis_size("fsdp")
    chips = ctx // 2
    my_ctx = lax.axis_index("ctx")
    my_fsdp = lax.axis_index("fsdp")
    info = jnp.stack([my_ctx, my_fsdp]).astype(jnp.int32)
    weight_rows = qkv_weight.shape[0]
    bias_width = qkv_bias.shape[0]
    own = gate_up_weight.shape[1] // 2 // ctx
    padded = -(-own // LANES) * LANES
    gain_one = norm1_gain.astype(F32)[:, None]
    gain_two = norm2_gain.astype(F32)[:, None]

    each = LANES // bias_width
    spot = (my_ctx * fsdp + my_fsdp) % each
    bias_row = jnp.where(
        jnp.arange(LANES, dtype=jnp.int32) // bias_width == spot, jnp.tile(qkv_bias, each), 0.0
    ).astype(BF16)
    bias_block = jnp.zeros((weight_rows, LANES), BF16).at[0].set(bias_row)
    packed = pl.pallas_call(
        pack_kernel,
        out_shape=struct((weight_rows, QKV + LANES + width), BF16),
        compiler_params=params(),
        name="pack",
    )(qkv_weight, bias_block, out_weight, gain_one)
    own_down = down_weight.shape[0]
    aligned = is_aligned(weight_rows, fsdp) and own_down % 8 == 0
    split = pl.pallas_call(
        functools.partial(split_kernel, own),
        out_shape=struct((ctx, weight_rows, 2 * padded), BF16),
        compiler_params=params(),
        name="split",
    )(gate_up_weight, after(gain_two, packed))
    bits = bits_of(fsdp)
    d_half = width // 2
    steps_half = jnp.arange(0, HEAD_DIM, 2).astype(F32)
    inverse = 10000.0 ** (-steps_half / HEAD_DIM)
    angles = positions[0].astype(F32)[:, None] * inverse[None, :]
    cosine = jnp.tile(jnp.cos(angles), (1, 2))
    sine = jnp.concatenate([-jnp.sin(angles), jnp.sin(angles)], axis=-1)
    places = positions[0][:, None]
    if aligned:
        pieces, plan, down_held, wide_part, last = gather_head(
            packed, down_weight, split, [cosine, sine, places], chips
        )
        w_down = call(
            functools.partial(stack_kernel, fsdp),
            struct((own, width), BF16),
            [info] + down_held,
            scratch=[pltpu.VMEM((own, width), F32)],
            estimate=cost(0, 0),
            name="stack",
        )
    else:
        pieces, plan, last = [lax.all_gather(packed, BOTH, axis=0, tiled=True)], None, []
        wide_part = lax.all_to_all(split, "ctx", 0, 0)
        w_down = lax.all_gather(down_weight, "fsdp", axis=0, tiled=True)
    gate_part, up_part = wide_part[:, :, :padded], wide_part[:, :, padded:]
    if aligned:
        gate_held, up_held = spread(gate_part, bits), spread(up_part, bits[::-1])
        items = sorted(gate_held)
        near_wide = [gate_held[bits[0]], up_held[bits[-1]]]
        wide_plan = [(index, block, item) for index, item in enumerate(items) for block in range(ctx)]
        wide_pieces = [gate_held[item] for item in items] + [up_held[item] for item in items]
    else:
        wide_plan = None
        near_wide = []
        wide_pieces = [
            lax.all_gather(part, "fsdp", axis=1, tiled=False).reshape(width, padded)
            for part in (gate_part, up_part)
        ]
    wide_count = len(wide_pieces) // 2
    all_cots = lax.all_gather(after(grad_out, *last), "ctx", axis=0, tiled=True)

    count = len(pieces)
    unit_one, queries, own_kv = call(
        functools.partial(project_kernel, plan, chips, fsdp, bias_width, count),
        [struct((rows, width), BF16), struct((rows, WIDTH_Q), BF16), struct((rows, 2 * WIDTH_K), BF16)],
        [info, inputs, cosine, sine] + pieces,
        4,
        4 + count,
        [pltpu.VMEM((width, QKV + LANES), BF16), pltpu.SemaphoreType.DMA((len(plan or [0]),))],
        cost(2 * rows * width * QKV, 2 * width * QKV),
        "project",
    )
    reach = -(-chips // 2)
    kv_blocks, sources = [], []
    for step in range(reach + 1):
        block = own_kv if step == 0 else shift_open(own_kv, step)
        kv_blocks += [block, swap_core(block)]
        sources += [(step, 0), (step, 1)]
    span = len(sources) * rows
    context, middle, unit_two = call(
        functools.partial(attend_kernel, plan, chips, fsdp, count, sources),
        [struct((rows, width), BF16), struct((rows, width), F32), struct((rows, width), BF16)],
        [after(info, *near_wide), places, queries, inputs] + kv_blocks + pieces,
        4 + len(sources),
        4 + len(sources) + count,
        [pltpu.VMEM((width, width), BF16), pltpu.SemaphoreType.DMA((len(plan or [0]),))],
        cost(4 * rows * span * WIDTH_Q + 2 * rows * width * width, 2 * width * width, rows * span * Q_HEADS),
        "attend",
    )

    all_units = lax.all_gather(after(unit_two, all_cots), "ctx", axis=0, tiled=True)
    order = list(range(2, chips - 1)) + [1, chips - 1, 0] if chips > 2 else list(range(chips))[::-1]
    hidden_grads = call(
        functools.partial(hidden_grad_kernel, order, chips, rows, padded),
        struct((ctx * rows, padded), BF16),
        [info, all_cots, w_down],
        estimate=cost(0, 0),
        name="hidden_grad",
    )
    turned = call(
        functools.partial(turn_kernel, order, chips, rows),
        struct((width, ctx * rows), BF16),
        [after(info, hidden_grads, *wide_pieces), all_units],
        estimate=cost(0, 4 * ctx * rows * width),
        name="turn",
    )
    half = len(order) // 2
    fed, unit_parts, when = [], {}, turned
    groups = (order[:half], order[half:])
    plan_count = len(wide_plan or [0])
    for steps in groups:
        tokens_now = 2 * rows * len(steps)
        mine, other, hidden, grads = call(
            functools.partial(
                feed_kernel, steps, 2 * rows * order.index(steps[0]), wide_plan, chips, fsdp, padded, wide_count
            ),
            [
                struct((len(steps), rows, width), BF16),
                struct((len(steps), rows, width), BF16),
                struct((padded, tokens_now), BF16),
                struct((tokens_now, 2 * padded), BF16),
            ],
            [after(info, when), all_units, hidden_grads] + wide_pieces,
            1,
            3 + 2 * wide_count,
            [
                pltpu.VMEM((tokens_now, width), BF16),
                pltpu.VMEM((tokens_now, padded), BF16),
                pltpu.VMEM((width, padded), BF16),
                pltpu.VMEM((width, padded), BF16),
                pltpu.VMEM((tokens_now, width), F32),
                pltpu.SemaphoreType.DMA((plan_count,)),
                pltpu.SemaphoreType.DMA((plan_count,)),
                pltpu.SemaphoreType.DMA((len(steps) + 1,)),
            ],
            cost(0, 0),
            "feed",
        )
        fed.append((hidden, grads))
        early = list(unit_parts.values())
        swapped = swap_core(after(other, *early))
        parts = sums(info, *[[(mine, index), (swapped, index)] for index in range(len(steps))])
        for step, part in zip(steps, parts):
            unit_parts[step] = shift_chip(part, -step) if step else part
        when = parts[0]

    n_block = 384 if padded % 384 == 0 else LANES

    def wide_grad(start, items, when):
        outs = 4 if items else 1
        shape = (fsdp // 2, chips, weight_rows, padded) if items else (fsdp, ctx, weight_rows, padded)
        return pl.pallas_call(
            functools.partial(wide_grad_kernel, items),
            out_shape=[struct(shape, BF16)] * outs,
            grid=(padded // n_block,),
            in_specs=[SMEM_SPEC, pl.BlockSpec((width, ctx * rows), lambda i: (0, 0))]
            + [
                pl.BlockSpec((grads.shape[0], n_block), lambda i: (0, start // n_block + i))
                for _, grads in fed
            ],
            out_specs=[pl.BlockSpec(shape[:3] + (n_block,), lambda i: (0, 0, 0, i))] * outs,
            scratch_shapes=[pltpu.VMEM((width, n_block), F32)],
            compiler_params=params(),
            cost_estimate=cost(2 * ctx * rows * width * padded, 4 * width * padded),
            name="wide_grad",
        )(when, turned, *[grads for _, grads in fed])

    turns = (bits, bits[::-1])
    wide_orders = [halving_order(items) for items in turns] if aligned else None
    gate_parts = wide_grad(0, wide_orders, after(info, *early))
    up_parts = wide_grad(padded, wide_orders, after(info, gate_parts[0]))

    def wide_first(parts, *waits):
        return [swap_fsdp(after(part, *waits), items[0]) for part, items in zip(parts[::2], turns)]

    def wide_second(parts, came, *waits):
        pairs = []
        for keep, more, items in zip(parts[1::2], came, turns):
            away = swap_fsdp(after(keep[0] + more[0], *waits), items[1])
            pairs.append((keep[1] + more[1], away))
        return pairs

    def wide_across(pairs, *waits):
        return lax.all_to_all(
            after(jnp.concatenate([mine + away for mine, away in pairs], axis=0), *waits), "ctx", 0, 0
        )

    gate_came = wide_first(gate_parts) if aligned else []
    up_came = wide_first(up_parts, *unit_parts.values()) if aligned else []

    grad_middle, grad_attention, grad_queries, kv_mine, kv_other = call(
        functools.partial(middle_back_kernel, plan, chips, fsdp, count, sources),
        [
            struct((rows, width), F32),
            struct((rows, width), BF16),
            struct((rows, WIDTH_Q), F32),
            struct((reach + 1, rows, 2 * WIDTH_K), BF16),
            struct((reach + 1, rows, 2 * WIDTH_K), BF16),
        ],
        [after(info, up_parts[0]), places, queries, middle, grad_out]
        + [unit_parts[step] for step in range(chips)]
        + kv_blocks
        + pieces,
        5 + chips + len(sources),
        5 + chips + len(sources) + count,
        [pltpu.VMEM((width, width), BF16), pltpu.SemaphoreType.DMA((len(plan or [0]),))],
        cost(10 * rows * span * WIDTH_Q + 2 * rows * width * width, 2 * width * width, rows * span * Q_HEADS),
        "middle_back",
    )
    halves = halves_of(chips, fsdp)

    def block_shapes(columns):
        if not aligned:
            return [struct((width, columns), BF16)]
        return 2 * [struct((fsdp, len(steps), weight_rows, columns), BF16) for steps, _ in halves]

    swapped = swap_core(after(kv_other, *gate_came))
    returned = [kv_mine[step] + swapped[step] for step in range(1, reach + 1)]
    branch = call(
        functools.partial(branch_kernel, groups, chips, rows),
        struct((ctx * rows, width), BF16),
        [after(info, *returned), w_down] + [hidden for hidden, _ in fed],
        estimate=cost(0, 0),
        name="branch",
    )
    gate_pairs = wide_second(gate_parts, gate_came, *returned) if aligned else []
    came = [shift_open(part, -step - 1) for step, part in enumerate(returned)]
    outs = call(
        functools.partial(projected_back_kernel, chips, fsdp, bias_width, reach),
        [struct((rows, QKV), BF16)] + block_shapes(QKV + LANES),
        [after(info, branch), grad_queries, kv_mine[0], swapped[0], cosine, sine, unit_one] + came,
        scratch=[pltpu.VMEM((width, QKV + LANES), F32)],
        estimate=cost(2 * rows * width * QKV, 2 * width * QKV),
        name="projected_back",
    )
    grad_projected, qkv_parts = outs[0], outs[1:]
    out_parts = call(
        functools.partial(out_grad_kernel, chips, fsdp),
        block_shapes(width),
        [after(info, grad_projected), grad_attention, context],
        scratch=[pltpu.VMEM((width, width), F32)],
        estimate=cost(2 * rows * width * width, 2 * width * width),
        name="out_grad",
    )
    def back_to_input(waits):
        return call(
            functools.partial(input_back_kernel, plan, chips, fsdp, count),
            struct((rows, width), F32),
            [after(info, *waits), grad_projected, inputs, grad_middle] + pieces,
            4,
            4 + count,
            [pltpu.VMEM((width, QKV), BF16), pltpu.SemaphoreType.DMA((len(plan or [0]),))],
            cost(2 * rows * width * QKV, 2 * width * QKV),
            "input_back",
        )

    (down_part,) = call(
        functools.partial(down_grad_kernel, None, order, chips, rows),
        [struct((own, width), BF16)],
        [after(info, out_parts[0], *[away for _, away in gate_pairs]), all_cots] + [hidden for hidden, _ in fed],
        scratch=[pltpu.VMEM((own, d_half), F32)],
        estimate=cost(0, 0),
        name="down_grad",
    )
    down_grad = lax.psum_scatter(down_part, "fsdp", scatter_dimension=0, tiled=True).astype(F32)

    if aligned:
        sides = [items for _, items in halves]

        def swapped_of(parts, *waits):
            return [(keep, swap_core(after(send, *waits))) for keep, send in zip(parts[:2], parts[2:])]

        def first_exchange(pairs, *waits):
            half = fsdp // 2
            return [
                swap_fsdp(after(keep[:half] + got[:half], *waits), items[0])
                for (keep, got), items in zip(pairs, sides)
            ]

        def second_exchange(pairs, came_back):
            sums = []
            for (keep, got), more, items in zip(pairs, came_back, sides):
                away = swap_fsdp(keep[2] + got[2] + more[0], items[1])
                sums.append((keep[3] + got[3] + more[1], away))
            return [mine + away for mine, away in sums]

        aways = [away for _, away in gate_pairs]
        up_pairs = wide_second(up_parts, up_came, *aways)
        gate_back = wide_across(gate_pairs, grad_projected)
        qkv_pairs = swapped_of(qkv_parts)
        qkv_came = first_exchange(qkv_pairs, *[away for _, away in up_pairs])
        input_grad = back_to_input([down_part, *[got for _, got in qkv_pairs]])
        up_back = wide_across(up_pairs, gate_back)
        out_pairs = swapped_of(out_parts)
        qkv_far = second_exchange(qkv_pairs, [after(item, input_grad) for item in qkv_came])
        out_came = first_exchange(out_pairs, *qkv_came)
        qkv_sum = reduce_chips(qkv_far, chips, fsdp)
        out_far = second_exchange(out_pairs, [after(item, *qkv_far) for item in out_came])
        out_grad = reduce_chips(out_far, chips, fsdp)
    else:

        def over(array, axes):
            return lax.psum_scatter(array, axes, scatter_dimension=0, tiled=True)

        qkv_sum, out_grad = (over(parts[0], BOTH).astype(F32) for parts in (qkv_parts, out_parts))
        gate_back, up_back = (
            lax.all_to_all(
                over(parts[0].reshape(-1, padded), "fsdp").reshape(ctx, weight_rows, padded), "ctx", 0, 0
            )
            for parts in (gate_parts, up_parts)
        )
        input_grad = back_to_input([])
    branch = lax.psum_scatter(branch, "ctx", scatter_dimension=0, tiled=True)
    result = (middle + branch.astype(F32)).astype(BF16)
    gate_up_grad, norm2_grad = pl.pallas_call(
        functools.partial(join_kernel, own),
        out_shape=[struct(gate_up_weight.shape, F32), struct((weight_rows, 1), F32)],
        compiler_params=params(),
        name="join",
    )(gate_back, up_back, gate_up_weight, after(gain_two, input_grad))
    bias_row = lax.dynamic_slice_in_dim(qkv_sum[0], QKV + spot * bias_width, bias_width)
    qkv_sum = qkv_sum[:, :QKV]
    return (
        result[None],
        input_grad[None],
        jnp.sum(qkv_sum * qkv_weight.astype(F32), axis=1),
        qkv_sum * gain_one,
        bias_row,
        out_grad,
        norm2_grad[:, 0],
        gate_up_grad,
        down_grad,
    )


def solution(mesh):
    rows = P(BOTH, None)
    token = P("fsdp", "ctx", None)
    flat = P(BOTH)
    return jax.shard_map(
        shards,
        mesh=mesh,
        in_specs=(token, P("fsdp", "ctx"), P("fsdp", "ctx"), flat, rows, flat, rows, flat, rows, rows, token),
        out_specs=(token, token, flat, rows, flat, rows, flat, rows, rows),
        check_vma=False,
    )
```
